256 devices in a mesh: rep: 16 (over x, z_hi, core), fsdp: 16 (over y, z_lo).
Axes of the slice: x: 4, y: 4, z: 8 (z_hi: 2, z_lo: 4; z = z_hi * 4 + z_lo), core: 2. Of those that a mesh axis runs over, the one named last changes fastest.
Arguments:
- tokens: bfloat16 [16, 4096, 4608], P('rep', 'fsdp'), may hold values from -240 to 240
- gain_offset: float32 [16, 4608], P('rep'), may hold values from -1.5 to 1.5
- key_weight: bfloat16 [16, 4608, 1024], P('rep', 'fsdp'), may hold values from -0.09375 to 0.09375
- key_cotangent: bfloat16 [16, 4096, 1024], P('rep', 'fsdp'), may hold values from -6 to 6
- outer_fragment: float32 [4608, 1024], P('fsdp'), may hold values from -6 to 6
- outer_momentum: float32 [4608, 1024], P('fsdp'), may hold values from -3 to 3
- inner_fragment: bfloat16 [16, 4608, 1024], P('rep', 'fsdp'), may hold values from -6 to 6
Outputs:
- input_grad: bfloat16 [16, 4096, 4608], P('rep', 'fsdp')
- gain_grad: float32 [16, 4608], P('rep')
- weight_grad: float32 [16, 4608, 1024], P('rep', 'fsdp')
- new_outer: float32 [4608, 1024], P('fsdp')
- new_momentum: float32 [4608, 1024], P('fsdp')
The draws below stay inside these ranges and needn't reach their ends.
All inputs are finite; a program needn't handle non-finite values.
Results may differ from the reference program's by a relative error of at most 0.012.
Values may be sent and summed in bfloat16 or wider, within the bound.
A program may use at most 128 MiB of HBM per device.

```python
import math
import jax
import jax.numpy as jnp
from jax import lax

D = 4608
KW = 1024
REPS = 16
TOKENS = 4096


def draw_tokens(key, part):
    key = jax.random.fold_in(key, 11)
    first, second, third = jax.random.split(key, 3)
    row_scales = jnp.exp(jax.random.uniform(first, (REPS, TOKENS, 1), jnp.float32) * math.log(10.0))
    column_scales = jnp.exp(jax.random.uniform(second, (1, 1, D), jnp.float32) * math.log(4.0))
    values = jnp.clip(jax.random.normal(third, (REPS, TOKENS, D), jnp.float32), -6.0, 6.0)
    return (values * row_scales * column_scales).astype(jnp.bfloat16)


def block_levels(own_key, dims, pieces, low, top_value):
    loudness, own = 1.0, jax.random.fold_in(own_key, 6)
    for axis_at, shards_of in pieces:
        draws = jnp.exp(jax.random.uniform(jax.random.fold_in(own, axis_at), (shards_of,), jnp.float32, low / len(pieces), top_value / len(pieces)))
        loudness = loudness * jnp.repeat(draws, dims[axis_at] // shards_of).reshape([-1 if axis == axis_at else 1 for axis in range(len(dims))])
    return loudness


def scatter_about(stream_key, shape, spread, most, pieces=(), kind=jnp.bfloat16):
    entries = spread * jax.random.normal(stream_key, shape, jnp.float32)
    if pieces:
        entries = entries * block_levels(stream_key, shape, pieces, -0.22, 0.18)
    return jnp.clip(entries, -most, most).astype(kind)


def setup_inputs(seed: int = 0) -> dict:
    keys = jax.random.split(jax.random.key(seed), 8)
    tokens = draw_tokens(jax.random.fold_in(keys[7], 71), 0)
    gain_offset = scatter_about(keys[1], (REPS, D), 0.3, 1.5, ((0, 16),), jnp.float32)
    key_weight = scatter_about(keys[2], (REPS, D, KW), D ** -0.5, 0.09375, ((0, 16), (1, 16)))
    key_cotangent = scatter_about(keys[3], (REPS, TOKENS, KW), 1.0, 6.0, ((0, 16), (1, 16)))
    outer_fragment = scatter_about(keys[4], (D, KW), 1.0, 6.0, ((0, 16),), jnp.float32)
    outer_momentum = scatter_about(keys[5], (D, KW), 0.5, 3.0, ((0, 16),), jnp.float32)
    inner_fragment = scatter_about(keys[6], (REPS, D, KW), 1.0, 6.0, ((0, 16), (1, 16)))
    return {"tokens": tokens, "gain_offset": gain_offset, "key_weight": key_weight, "key_cotangent": key_cotangent, "outer_fragment": outer_fragment, "outer_momentum": outer_momentum, "inner_fragment": inner_fragment}


EPSILON = 1e-06
OUTER_RATE = 0.7
MOMENTUM = 0.9

def replica_step(packed):
    tokens, gain_offset, key_weight, key_cotangent = packed
    source = tokens.astype(jnp.float32)
    inverse = lax.rsqrt(lax.optimization_barrier(jnp.mean(source * source, axis=1, keepdims=True)) + EPSILON)
    unit = source * inverse
    factor = 1.0 + gain_offset
    normed = (unit * factor).astype(jnp.bfloat16)
    weight_grad = jnp.dot(normed.T, key_cotangent, preferred_element_type=jnp.float32)
    feature_grad = jnp.dot(key_cotangent, key_weight.T, preferred_element_type=jnp.float32).astype(jnp.bfloat16)
    grad_float = feature_grad.astype(jnp.float32)
    gain_grad = lax.optimization_barrier(jnp.sum(grad_float * unit, axis=0))
    scaled = grad_float * factor
    projected = lax.optimization_barrier(jnp.mean(scaled * unit, axis=1, keepdims=True))
    input_grad = (inverse * (scaled - unit * projected)).astype(jnp.bfloat16)
    return (input_grad, gain_grad, weight_grad)

def reference(tokens, gain_offset, key_weight, key_cotangent, outer_fragment, outer_momentum, inner_fragment):
    input_grad, gain_grad, weight_grad = lax.map(replica_step, (tokens, gain_offset, key_weight, key_cotangent))
    differences = outer_fragment[None] - inner_fragment.astype(jnp.float32)
    pseudo = lax.optimization_barrier(jnp.sum(differences, axis=0)) / REPS
    new_momentum = MOMENTUM * outer_momentum + pseudo
    new_outer = outer_fragment - OUTER_RATE * (pseudo + MOMENTUM * new_momentum)
    return (input_grad, gain_grad, weight_grad, new_outer, new_momentum)
```

```python
import jax
import jax.numpy as jnp
from jax import lax
from jax.experimental import pallas as pl
from jax.experimental.pallas import tpu as pltpu
from jax.sharding import PartitionSpec as P

EPSILON = 1e-06
OUTER_RATE = 0.7
MOMENTUM = 0.9

MESH = pl.DeviceIdType.MESH
F32 = jnp.float32
BF16 = jnp.bfloat16

D = 4608
KW = 1024
ROWS = 256
SHARD = 288
BLOCK = 1152
CHUNK = 384
NCHUNK = 3
REPS = 16
PIECES = 4
PIECE = ROWS // PIECES
LANE = 128

WITH_FSDP = True
WITH_REP = True


def kernel(
    tokens,
    gain,
    weight,
    cotangent,
    outer,
    momentum,
    inner,
    input_grad,
    gain_grad,
    weight_grad,
    new_outer,
    new_momentum,
    tok_v,
    gain_v,
    cx,
    wx,
    tx,
    rs_own,
    rsx,
    rb,
    nt,
    gp,
    sb,
    ru,
    rd,
    wg_v,
    fx,
    fin,
    ig_v,
    gz,
    gy,
    gg_v,
    outer_v,
    mom_v,
    inner_v,
    db,
    cr,
    s1,
    xr,
    zs,
    zr,
    xs,
    no_v,
    nm_v,
    loc,
    tok_loc,
    out_sem,
    c_s,
    c_r,
    t_s,
    t_r,
    r_s,
    r_r,
    w_s,
    w_f,
    w_r,
    g_s,
    u_r,
    d_r,
    f_s,
    f_r,
    gz_s,
    gz_r,
    gy_s,
    gy_r,
    k_s,
    k_r,
    x_s,
    x_r,
    h_s,
    h_r,
):
    fi = lax.axis_index("fsdp")
    ri = lax.axis_index("rep")
    y, z = fi // 4, lax.rem(fi, 4)
    x, zh, core = ri // 4, lax.rem(ri // 2, 2), lax.rem(ri, 2)

    def y_peer(d):
        return (ri, lax.rem(y + d, 4) * 4 + z)

    def z_peer(to):
        return (ri, y * 4 + to)

    def x_peer(d):
        return (lax.rem(x + d, 4) * 4 + zh * 2 + core, fi)

    h_peer = (x * 4 + (1 - zh) * 2 + core, fi)
    core_peer = (x * 4 + zh * 2 + (1 - core), fi)

    def remote(src, dst, send, recv, peer):
        return pltpu.make_async_remote_copy(
            src_ref=src, dst_ref=dst, send_sem=send, recv_sem=recv, device_id=peer, device_id_type=MESH
        )

    def local(src, dst, sem):
        copy = pltpu.make_async_copy(src, dst, sem)
        copy.start()
        return copy

    def chunk_at(step):
        return jnp.where(z < 2, NCHUNK - 1 - step, step)

    def chunk_columns(block, chunk):
        return pl.ds(pl.multiple_of(block * BLOCK + chunk * CHUNK, LANE), CHUNK)

    def shard_rows(j):
        return pl.ds(pl.multiple_of(j * SHARD, 32), SHARD)

    copies = {}
    if WITH_FSDP:
        copies["tokens"] = local(tokens.at[0], tok_v, loc.at[0])
        copies["gain"] = local(gain, gain_v, loc.at[1])
        copies["c"] = local(cotangent.at[0], cx.at[y], loc.at[2])
        copies["w"] = local(weight.at[0], wx.at[shard_rows(z)], loc.at[3])
        for step in range(NCHUNK):
            chunk = chunk_at(step)
            copies["t", step] = local(
                tokens.at[0, :, chunk_columns(y, chunk)], tx.at[chunk, y], tok_loc.at[step]
            )
    if WITH_REP:
        copies["outer"] = local(outer, outer_v, loc.at[4])
        copies["momentum"] = local(momentum, mom_v, loc.at[5])
        copies["inner"] = local(inner.at[0], inner_v, loc.at[6])

    barrier = pltpu.get_barrier_semaphore()
    peers = []
    if WITH_FSDP:
        peers += [y_peer(d) for d in (1, 2, 3)] + [z_peer(lax.rem(z + d, 4)) for d in (1, 2, 3)]
    if WITH_REP:
        peers += [x_peer(d) for d in (1, 2, 3)] + [h_peer, core_peer]
    for peer in peers:
        pl.semaphore_signal(barrier, inc=1, device_id=peer, device_id_type=MESH)
    pl.semaphore_wait(barrier, len(peers))

    sends = []

    def start(copy):
        copy.start()
        sends.append(copy)
        return copy

    def c_copy(i):
        if i == 0:
            return remote(cotangent.at[0], cx.at[y], c_s.at[0], c_r.at[0], y_peer(1))
        if i == 1:
            return remote(cotangent.at[0], cx.at[y], c_s.at[1], c_r.at[1], y_peer(3))
        if i == 2:
            half = cx.at[lax.rem(y + 3, 4), pl.ds(0, ROWS // 2)]
            return remote(half, half, c_s.at[2], c_r.at[2], y_peer(1))
        half = cx.at[lax.rem(y + 1, 4), pl.ds(ROWS // 2, ROWS // 2)]
        return remote(half, half, c_s.at[3], c_r.at[3], y_peer(3))

    def t_copy(step, d):
        chunk = chunk_at(step)
        return remote(
            tokens.at[0, :, chunk_columns(lax.rem(y + d, 4), chunk)],
            tx.at[chunk, y],
            t_s.at[step, d - 1],
            t_r.at[step, d - 1],
            y_peer(d),
        )

    def start_tokens(step):
        for d in (1, 3, 2):
            start(t_copy(step, d))

    def r_copy(d):
        return remote(rsx.at[y], rsx.at[y], r_s.at[d - 1], r_r.at[d - 1], y_peer(d))

    up, down = jnp.minimum(z + 1, 3), jnp.maximum(z - 1, 0)

    def w_own(i):
        to = up if i == 0 else down
        return remote(weight.at[0], wx.at[shard_rows(z)], w_s.at[i], w_r.at[z], z_peer(to))

    def w_forward(j, to):
        rows = wx.at[shard_rows(j)]
        return remote(rows, rows, w_f.at[j], w_r.at[j], z_peer(to))

    def weight_step(s):
        @pl.when(z >= s)
        def _():
            w_forward(z - s, up).wait_recv()

            @pl.when(z < 3)
            def _():
                w_forward(z - s, up).start()

        @pl.when(z + s <= 3)
        def _():
            w_forward(z + s, down).wait_recv()

            @pl.when(z > 0)
            def _():
                w_forward(z + s, down).start()

    def g_up(j):
        return remote(sb.at[j], ru.at[j], g_s.at[j], u_r.at[j], z_peer(up))

    def g_down(j):
        return remote(sb.at[j], rd.at[j], g_s.at[j], d_r.at[j], z_peer(down))

    def send_sum(j, arrived, copy, first):
        def add(i, _):
            rows = pl.ds(pl.multiple_of(i * 32, 32), 32)
            part = gp[pl.ds(pl.multiple_of(j * SHARD + i * 32, 32), 32), :]
            if not first:
                part = part + arrived[j, rows, :].astype(F32)
            sb[j, rows, :] = part.astype(BF16)
            return 0

        if not first:
            copy(j).wait_recv()
        lax.fori_loop(0, SHARD // 32, add, 0)
        copy(j).start()

    def sums_up(j, first):
        send_sum(j, ru, g_up, first)

    def sums_down(j, first):
        send_sum(j, rd, g_down, first)

    def sum_step(s):
        if s == 1:

            @pl.when(z == 0)
            def _():
                sums_up(3, True)

            @pl.when(z == 3)
            def _():
                sums_down(0, True)
        elif s == 2:

            @pl.when(z == 0)
            def _():
                sums_up(2, True)

            @pl.when(z == 3)
            def _():
                sums_down(1, True)

            @pl.when(z == 1)
            def _():
                sums_up(3, False)

            @pl.when(z == 2)
            def _():
                sums_down(0, False)
        else:

            @pl.when(z == 0)
            def _():
                sums_up(1, True)

            @pl.when(z == 3)
            def _():
                sums_down(2, True)

            @pl.when(z == 1)
            def _():
                sums_up(2, False)
                sums_down(0, False)

            @pl.when(z == 2)
            def _():
                sums_down(1, False)
                sums_up(3, False)

    def sum_last():
        @pl.when(z > 0)
        def _():
            g_up(z).wait_recv()

        @pl.when(z < 3)
        def _():
            g_down(z).wait_recv()

        def add(i, _):
            rows = pl.ds(pl.multiple_of(i * 32, 32), 32)
            wg_v[rows, :] = gp[pl.ds(pl.multiple_of(z * SHARD + i * 32, 32), 32), :]

            @pl.when(z > 0)
            def _():
                wg_v[rows, :] += ru[z, rows, :].astype(F32)

            @pl.when(z < 3)
            def _():
                wg_v[rows, :] += rd[z, rows, :].astype(F32)

            return 0

        lax.fori_loop(0, SHARD // 32, add, 0)
        copies["weight_grad"] = local(wg_v, weight_grad.at[0], out_sem.at[0])

    def f_copy(piece, d):
        to = lax.rem(y + d, 4)
        rows = pl.ds(piece * PIECE, PIECE)
        return remote(
            fx.at[:, to, rows],
            fin.at[y, :, rows],
            f_s.at[piece, d - 1],
            f_r.at[piece, d - 1],
            y_peer(d),
        )

    def start_features(piece):
        for d in (1, 3, 2):
            start(f_copy(piece, d))

    def gz_copy(d):
        return remote(gz.at[z], gz.at[z], gz_s.at[d - 1], gz_r.at[d - 1], z_peer(lax.rem(z + d, 4)))

    def gy_copy(d):
        return remote(gy.at[y], gy.at[y], gy_s.at[d - 1], gy_r.at[d - 1], y_peer(d))

    def k_copy(i):
        if i == 0:
            return remote(db.at[pl.ds((1 - core) * 4, 4)], cr, k_s.at[0], k_r.at[0], core_peer)
        part = xs.at[pl.ds(core * 4, 4)]
        return remote(part, part, k_s.at[1], k_r.at[1], core_peer)

    def x_copy(i, d):
        if i == 0:
            return remote(
                s1.at[lax.rem(x + d, 4)], xr.at[d - 1], x_s.at[0, d - 1], x_r.at[0, d - 1], x_peer(d)
            )
        part = xs.at[core * 4 + x]
        return remote(part, part, x_s.at[1, d - 1], x_r.at[1, d - 1], x_peer(d))

    def h_copy():
        return remote(zs, zr, h_s, h_r, h_peer)

    def inverse_root():
        def body(i, _):
            rows = pl.ds(pl.multiple_of(i * 16, 16), 16)
            total = jnp.zeros((16, LANE), F32)
            for j in range(D // LANE):
                v = tok_v[rows, j * LANE : (j + 1) * LANE].astype(F32)
                total = total + v * v
            mean = jnp.sum(total, axis=1, keepdims=True) / D
            rs_own[rows, :] = jnp.broadcast_to(lax.rsqrt(mean + EPSILON), (16, LANE))
            return 0

        lax.fori_loop(0, ROWS // 16, body, 0)
        rsx[y] = jnp.transpose(rs_own[...])[0:8, :]

    def spread_roots():
        def body(s, _):
            rb[s] = jnp.transpose(jnp.broadcast_to(rsx[s][0:1, :], (LANE, ROWS)))
            return 0

        lax.fori_loop(0, 4, body, 0)

    def weight_chunk(chunk):
        def norm(s, _):
            for q in range(CHUNK // LANE):
                unit = tx[chunk, s, :, q * LANE : (q + 1) * LANE].astype(F32) * rb[s]
                at = pl.multiple_of(y * BLOCK + chunk * CHUNK + q * LANE, LANE)
                normed = (unit * (1.0 + gain_v[0:1, pl.ds(at, LANE)])).astype(BF16)
                nt[s, q * LANE : (q + 1) * LANE, :] = jnp.transpose(normed)
            return 0

        lax.fori_loop(0, 4, norm, 0)

        def multiply(j, _):
            columns = pl.ds(pl.multiple_of(j * 256, 256), 256)
            total = jnp.zeros((CHUNK, 256), F32)
            for s in range(4):
                total = total + jnp.dot(nt[s], cx[s, :, columns], preferred_element_type=F32)
            gp[pl.ds(pl.multiple_of(chunk * CHUNK, CHUNK), CHUNK), columns] = total
            return 0

        lax.fori_loop(0, KW // 256, multiply, 0)

    def features():
        def body(i, _):
            t, s = i // 4, lax.rem(i, 4)
            product = lax.dot_general(
                cx[s],
                wx[pl.ds(pl.multiple_of(t * CHUNK, CHUNK), CHUNK), :],
                (((1,), (1,)), ((), ())),
                preferred_element_type=F32,
            )
            fx[t, s] = product.astype(BF16)
            return 0

        lax.fori_loop(0, NCHUNK * 4, body, 0)

    def gain_part():
        gz[z] = jnp.zeros((16, LANE), F32)

        def body(t, _):
            for q in range(CHUNK // LANE):
                lanes = slice(q * LANE, (q + 1) * LANE)

                def add(s, total):
                    unit = tx[t, s, :, lanes].astype(F32) * rb[s]
                    term = fx[t, s, :, lanes].astype(F32) * unit
                    return total + jnp.sum(term.reshape(ROWS // 8, 8, LANE), axis=0)

                total = lax.fori_loop(0, 4, add, jnp.zeros((8, LANE), F32))
                gz[z, pl.ds(t * (CHUNK // LANE) + q, 1), :] = jnp.sum(total, axis=0, keepdims=True)
            return 0

        lax.fori_loop(0, NCHUNK, body, 0)

    def input_piece(piece):
        def body(i, _):
            rows = pl.ds(pl.multiple_of(piece * PIECE + i * 16, 16), 16)
            root = rs_own[rows, :]

            def terms(s, t, q):
                at = s * BLOCK + t * CHUNK + q * LANE
                grad = fin[s, t, rows, q * LANE : (q + 1) * LANE].astype(F32)
                unit = tok_v[rows, at : at + LANE].astype(F32) * root
                return at, grad * (1.0 + gain_v[0:1, at : at + LANE]), unit

            places = [(s, t, q) for s in range(4) for t in range(NCHUNK) for q in range(CHUNK // LANE)]
            total = jnp.zeros((16, LANE), F32)
            for place in places:
                _, scaled, unit = terms(*place)
                total = total + scaled * unit
            projected = jnp.sum(total, axis=1, keepdims=True) / D
            for place in places:
                at, scaled, unit = terms(*place)
                ig_v[rows, at : at + LANE] = (root * (scaled - unit * projected)).astype(BF16)
            return 0

        lax.fori_loop(0, PIECE // 16, body, 0)
        rows = pl.ds(piece * PIECE, PIECE)
        copies["ig", piece] = local(ig_v.at[rows], input_grad.at[0, rows], out_sem.at[1 + piece])

    if WITH_FSDP:
        start(c_copy(0))
        start(c_copy(1))

        @pl.when(z < 3)
        def _():
            w_own(0).start()

        @pl.when(z > 0)
        def _():
            w_own(1).start()

        start_tokens(0)

    if WITH_REP:
        copies["outer"].wait()
        copies["inner"].wait()
        for b in range(8):
            lanes = slice(b * LANE, (b + 1) * LANE)
            db[b] = outer_v[:, lanes] - inner_v[:, lanes].astype(F32)
        start(k_copy(0))

    if WITH_FSDP:
        copies["tokens"].wait()
        inverse_root()
        for d in (1, 2, 3):
            start(r_copy(d))

    if WITH_REP:
        k_copy(0).wait_recv()
        for q in range(4):
            s1[q] = db[core * 4 + q] + cr[q]
        for d in (1, 2, 3):
            start(x_copy(0, d))
        for d in (1, 2, 3):
            x_copy(0, d).wait_recv()
        zs[...] = (s1[x] + xr[0] + xr[1] + xr[2]).astype(BF16)
        start(h_copy())

    if WITH_FSDP:
        c_copy(0).wait_recv()
        c_copy(1).wait_recv()
        start(c_copy(2))
        start(c_copy(3))
        start_tokens(1)
        weight_step(1)

    if WITH_REP:
        h_copy().wait_recv()
        xs[core * 4 + x] = zs[...].astype(F32) + zr[...].astype(F32)
        for d in (1, 2, 3):
            start(x_copy(1, d))
        for d in (1, 2, 3):
            x_copy(1, d).wait_recv()
        start(k_copy(1))

    if WITH_FSDP:
        copies["gain"].wait()
        for d in (1, 2, 3):
            r_copy(d).wait_recv()
        spread_roots()
        copies["c"].wait()
        copies["t", 0].wait()
        for d in (1, 2, 3):
            t_copy(0, d).wait_recv()
        start_tokens(2)
        c_copy(2).wait_recv()
        c_copy(3).wait_recv()
        weight_chunk(chunk_at(0))
        sum_step(1)
        weight_step(2)

    if WITH_REP:
        copies["momentum"].wait()
        k_copy(1).wait_recv()
        for b in range(8):
            lanes = slice(b * LANE, (b + 1) * LANE)
            pseudo = xs[b] / REPS
            momentum_next = MOMENTUM * mom_v[:, lanes] + pseudo
            nm_v[:, lanes] = momentum_next
            no_v[:, lanes] = outer_v[:, lanes] - OUTER_RATE * (pseudo + MOMENTUM * momentum_next)
        copies["new_outer"] = local(no_v, new_outer, out_sem.at[5])
        copies["new_momentum"] = local(nm_v, new_momentum, out_sem.at[6])

    if WITH_FSDP:
        copies["t", 1].wait()
        for d in (1, 2, 3):
            t_copy(1, d).wait_recv()
        weight_chunk(chunk_at(1))
        copies["w"].wait()
        weight_step(3)
        features()
        start_features(0)
        start_features(1)
        own = local(fx.at[:, y], fin.at[y], loc.at[7])
        sum_step(2)
        copies["t", 2].wait()
        for d in (1, 2, 3):
            t_copy(2, d).wait_recv()
        weight_chunk(chunk_at(2))
        gain_part()
        for d in (1, 2, 3):
            start(gz_copy(d))
        own.wait()
        for piece in range(PIECES):
            for d in (1, 2, 3):
                f_copy(piece, d).wait_recv()
            if piece + 2 < PIECES:
                start_features(piece + 2)
            input_piece(piece)
            if piece == 0:
                for d in (1, 2, 3):
                    gz_copy(d).wait_recv()
                gy[y] = gz[0] + gz[1] + gz[2] + gz[3]
                for d in (1, 2, 3):
                    start(gy_copy(d))
                sum_step(3)
            if piece == 1:
                for d in (1, 2, 3):
                    gy_copy(d).wait_recv()
                for b in range(4):
                    for i in range(BLOCK // LANE):
                        at = b * BLOCK + i * LANE
                        gg_v[0:1, at : at + LANE] = gy[b, i : i + 1, :]
                copies["gain_grad"] = local(gg_v, gain_grad, out_sem.at[7])
            if piece == 2:
                sum_last()

    for copy in sends:
        copy.wait_send()
    if WITH_FSDP:

        @pl.when(z < 3)
        def _():
            w_own(0).wait_send()

        @pl.when(z > 0)
        def _():
            w_own(1).wait_send()

        for s in (1, 2):

            @pl.when((z >= s) & (z < 3))
            def _():
                w_forward(z - s, up).wait_send()

            @pl.when((z + s <= 3) & (z > 0))
            def _():
                w_forward(z + s, down).wait_send()

        for d in (1, 2, 3):
            g_up(lax.rem(z + d, 4)).wait_send()
        copies["weight_grad"].wait()
        copies["gain_grad"].wait()
        for piece in range(PIECES):
            copies["ig", piece].wait()
    if WITH_REP:
        copies["new_outer"].wait()
        copies["new_momentum"].wait()


def call(*args):
    shapes = (
        jax.ShapeDtypeStruct((1, ROWS, D), BF16),
        jax.ShapeDtypeStruct((1, D), F32),
        jax.ShapeDtypeStruct((1, SHARD, KW), F32),
        jax.ShapeDtypeStruct((SHARD, KW), F32),
        jax.ShapeDtypeStruct((SHARD, KW), F32),
    )
    dma = pltpu.SemaphoreType.DMA
    scratch = [
        pltpu.VMEM((ROWS, D), BF16),
        pltpu.VMEM((1, D), F32),
        pltpu.VMEM((4, ROWS, KW), BF16),
        pltpu.VMEM((BLOCK, KW), BF16),
        pltpu.VMEM((NCHUNK, 4, ROWS, CHUNK), BF16),
        pltpu.VMEM((ROWS, LANE), F32),
        pltpu.VMEM((4, 8, ROWS), F32),
        pltpu.VMEM((4, ROWS, LANE), F32),
        pltpu.VMEM((4, CHUNK, ROWS), BF16),
        pltpu.VMEM((BLOCK, KW), F32),
        pltpu.VMEM((4, SHARD, KW), BF16),
        pltpu.VMEM((4, SHARD, KW), BF16),
        pltpu.VMEM((4, SHARD, KW), BF16),
        pltpu.VMEM((SHARD, KW), F32),
        pltpu.VMEM((NCHUNK, 4, ROWS, CHUNK), BF16),
        pltpu.VMEM((4, NCHUNK, ROWS, CHUNK), BF16),
        pltpu.VMEM((ROWS, D), BF16),
        pltpu.VMEM((4, 16, LANE), F32),
        pltpu.VMEM((4, 16, LANE), F32),
        pltpu.VMEM((1, D), F32),
        pltpu.VMEM((SHARD, KW), F32),
        pltpu.VMEM((SHARD, KW), F32),
        pltpu.VMEM((SHARD, KW), BF16),
        pltpu.VMEM((8, SHARD, LANE), F32),
        pltpu.VMEM((4, SHARD, LANE), F32),
        pltpu.VMEM((4, SHARD, LANE), F32),
        pltpu.VMEM((3, SHARD, LANE), F32),
        pltpu.VMEM((SHARD, LANE), BF16),
        pltpu.VMEM((SHARD, LANE), BF16),
        pltpu.VMEM((8, SHARD, LANE), F32),
        pltpu.VMEM((SHARD, KW), F32),
        pltpu.VMEM((SHARD, KW), F32),
        dma((8,)),
        dma((NCHUNK,)),
        dma((8,)),
        dma((4,)),
        dma((4,)),
        dma((NCHUNK, 3)),
        dma((NCHUNK, 3)),
        dma((3,)),
        dma((3,)),
        dma((2,)),
        dma((4,)),
        dma((4,)),
        dma((4,)),
        dma((4,)),
        dma((4,)),
        dma((PIECES, 3)),
        dma((PIECES, 3)),
        dma((3,)),
        dma((3,)),
        dma((3,)),
        dma((3,)),
        dma((2,)),
        dma((2,)),
        dma((2, 3)),
        dma((2, 3)),
        dma,
        dma,
    ]
    anywhere = pl.BlockSpec(memory_space=pl.ANY)
    return pl.pallas_call(
        kernel,
        out_shape=shapes,
        in_specs=[anywhere] * 7,
        out_specs=[anywhere] * 5,
        scratch_shapes=scratch,
        compiler_params=pltpu.CompilerParams(
            collective_id=0, has_side_effects=True, vmem_limit_bytes=60 * 2**20
        ),
        cost_estimate=pl.CostEstimate(
            flops=4 * ROWS * D * KW, bytes_accessed=16 * 2**20, transcendentals=ROWS
        ),
        name="inner_outer_step",
    )(*args)


def solution(mesh):
    return jax.shard_map(
        call,
        mesh=mesh,
        in_specs=(
            P("rep", "fsdp", None),
            P("rep", None),
            P("rep", "fsdp", None),
            P("rep", "fsdp", None),
            P("fsdp", None),
            P("fsdp", None),
            P("rep", "fsdp", None),
        ),
        out_specs=(
            P("rep", "fsdp", None),
            P("rep", None),
            P("rep", "fsdp", None),
            P("fsdp", None),
            P("fsdp", None),
        ),
        check_vma=False,
    )
```

```python
import jax
import jax.numpy as jnp
from jax import lax
from jax.experimental import pallas as pl
from jax.experimental.pallas import tpu as pltpu
from jax.sharding import PartitionSpec as P

EPSILON = 1e-06
OUTER_RATE = 0.7
MOMENTUM = 0.9

MESH = pl.DeviceIdType.MESH
F32 = jnp.float32
BF16 = jnp.bfloat16

D = 4608
KW = 1024
ROWS = 256
SHARD = 288
BLOCK = 1152
CHUNK = 384
NCHUNK = 3
REPS = 16
PIECES = 4
PIECE = ROWS // PIECES
HALF = ROWS // 2
PART = SHARD // 2
LANE = 128
VMEM_LIMIT = 48 * 2**20

WITH_FSDP = True
WITH_REP = True


def kernel(
    tokens,
    gain,
    weight,
    cotangent,
    outer,
    momentum,
    inner,
    ig_v,
    gg_v,
    wg_v,
    no_v,
    nm_v,
    tok_v,
    gain_v,
    cx,
    wx,
    tx,
    rs_own,
    rsx,
    rb,
    nt,
    gp,
    sb,
    ru,
    rd,
    fx,
    fin,
    gz,
    gy,
    outer_v,
    mom_v,
    inner_v,
    db,
    cr,
    s1,
    xr,
    zs,
    zr,
    xs,
    loc,
    tok_loc,
    c_s,
    c_r,
    t_s,
    t_r,
    r_s,
    r_r,
    w_s,
    w_f,
    w_r,
    g_s,
    u_r,
    d_r,
    f_s,
    f_r,
    p_s,
    p_r,
    gz_s,
    gz_r,
    gy_s,
    gy_r,
    k_s,
    k_r,
    x_s,
    x_r,
    h_s,
    h_r,
):
    fi = lax.axis_index("fsdp")
    ri = lax.axis_index("rep")
    y, z = fi // 4, lax.rem(fi, 4)
    x, zh, core = ri // 4, lax.rem(ri // 2, 2), lax.rem(ri, 2)

    def y_peer(d):
        return (ri, lax.rem(y + d, 4) * 4 + z)

    def z_peer(to):
        return (ri, y * 4 + to)

    def x_peer(d):
        return (lax.rem(x + d, 4) * 4 + zh * 2 + core, fi)

    h_peer = (x * 4 + (1 - zh) * 2 + core, fi)
    core_peer = (x * 4 + zh * 2 + (1 - core), fi)

    def remote(src, dst, send, recv, peer):
        return pltpu.make_async_remote_copy(
            src_ref=src, dst_ref=dst, send_sem=send, recv_sem=recv, device_id=peer, device_id_type=MESH
        )

    def local(src, dst, sem):
        copy = pltpu.make_async_copy(src, dst, sem)
        copy.start()
        return copy

    def chunk_at(step):
        return jnp.where(z < 2, NCHUNK - 1 - step, step)

    def chunk_columns(block, chunk):
        return pl.ds(pl.multiple_of(block * BLOCK + chunk * CHUNK, LANE), CHUNK)

    def shard_rows(j):
        return pl.ds(pl.multiple_of(j * SHARD, 32), SHARD)

    copies = {}
    if WITH_FSDP:
        copies["tokens"] = local(tokens.at[0], tok_v, loc.at[0])
    if WITH_REP:
        copies["outer"] = local(outer, outer_v, loc.at[4])
        copies["inner"] = local(inner.at[0], inner_v, loc.at[6])

    barrier = pltpu.get_barrier_semaphore()
    peers = []
    if WITH_FSDP:
        peers += [y_peer(d) for d in (1, 2, 3)] + [z_peer(lax.rem(z + d, 4)) for d in (1, 2, 3)]
    if WITH_REP:
        peers += [x_peer(d) for d in (1, 2, 3)] + [h_peer, core_peer]
    for peer in peers:
        pl.semaphore_signal(barrier, inc=1, device_id=peer, device_id_type=MESH)
    pl.semaphore_wait(barrier, len(peers))

    sends = []

    def start(copy):
        copy.start()
        sends.append(copy)
        return copy

    def c_copy(i):
        first, second = pl.ds(0, HALF), pl.ds(HALF, HALF)
        if i < 4:
            rows = first if i in (0, 3) else second
            at = cx.at[y, rows]
            return remote(cotangent.at[0, rows], at, c_s.at[i], c_r.at[i], y_peer(1 if i in (0, 2) else 3))
        if i == 4:
            part = cx.at[lax.rem(y + 3, 4), first]
            return remote(part, part, c_s.at[4], c_r.at[4], y_peer(1))
        part = cx.at[lax.rem(y + 1, 4), second]
        return remote(part, part, c_s.at[5], c_r.at[5], y_peer(3))

    def t_copy(step, d):
        chunk = chunk_at(step)
        return remote(
            tokens.at[0, :, chunk_columns(lax.rem(y + d, 4), chunk)],
            tx.at[chunk, y],
            t_s.at[step, d - 1],
            t_r.at[step, d - 1],
            y_peer(d),
        )

    def r_copy(d):
        return remote(rsx.at[y], rsx.at[y], r_s.at[d - 1], r_r.at[d - 1], y_peer(d))

    up, down = jnp.minimum(z + 1, 3), jnp.maximum(z - 1, 0)

    def w_own(i):
        to = up if i == 0 else down
        return remote(weight.at[0], wx.at[shard_rows(z)], w_s.at[i], w_r.at[z], z_peer(to))

    def w_forward(j, to):
        rows = wx.at[shard_rows(j)]
        return remote(rows, rows, w_f.at[j], w_r.at[j], z_peer(to))

    def weight_step(s):
        @pl.when(z >= s)
        def _():
            w_forward(z - s, up).wait_recv()

            @pl.when(z < 3)
            def _():
                w_forward(z - s, up).start()

        @pl.when(z + s <= 3)
        def _():
            w_forward(z + s, down).wait_recv()

            @pl.when(z > 0)
            def _():
                w_forward(z + s, down).start()

    def g_up(j, part):
        at = (j, pl.ds(part * PART, PART))
        return remote(sb.at[at], ru.at[at], g_s.at[j, part], u_r.at[j, part], z_peer(up))

    def g_down(j, part):
        at = (j, pl.ds(part * PART, PART))
        return remote(sb.at[at], rd.at[at], g_s.at[j, part], d_r.at[j, part], z_peer(down))

    def send_sum(j, part, arrived, copy, first):
        def add(i, _):
            at = part * PART + i * 16
            rows = pl.ds(pl.multiple_of(at, 16), 16)
            total = gp[pl.ds(pl.multiple_of(j * SHARD + at, 16), 16), :]
            if not first:
                total = total + arrived[j, rows, :].astype(F32)
            sb[j, rows, :] = total.astype(BF16)
            return 0

        if not first:
            copy(j, part).wait_recv()
        lax.fori_loop(0, PART // 16, add, 0)
        copy(j, part).start()

    def begin_sums(step):
        @pl.when(z == 0)
        def _():
            for part in range(2):
                send_sum(3 - step, part, ru, g_up, True)

        @pl.when(z == 3)
        def _():
            for part in range(2):
                send_sum(step, part, rd, g_down, True)

    def pass_sums(step, part):
        routes = (((3, ru, g_up), (0, rd, g_down)), ((0, rd, g_down), (3, ru, g_up)), ((2, ru, g_up), (1, rd, g_down)))
        for at, (j, arrived, copy) in zip((1, 2), routes[step]):

            @pl.when(z == at)
            def _():
                send_sum(j, part, arrived, copy, False)

    def end_sums(part):
        @pl.when(z > 0)
        def _():
            g_up(z, part).wait_recv()

        @pl.when(z < 3)
        def _():
            g_down(z, part).wait_recv()

        def add(i, _):
            at = part * PART + i * 16
            rows = pl.ds(pl.multiple_of(at, 16), 16)
            wg_v[0, rows, :] = gp[pl.ds(pl.multiple_of(z * SHARD + at, 16), 16), :]

            @pl.when(z > 0)
            def _():
                wg_v[0, rows, :] += ru[z, rows, :].astype(F32)

            @pl.when(z < 3)
            def _():
                wg_v[0, rows, :] += rd[z, rows, :].astype(F32)

            return 0

        lax.fori_loop(0, PART // 16, add, 0)

    def feature_chunk(step):
        return jnp.where(z < 2, step, NCHUNK - 1 - step)

    def f_copy(step, d):
        chunk = feature_chunk(step)
        to = lax.rem(y + d, 4)
        return remote(fx.at[chunk, to], fin.at[y, chunk], f_s.at[step, d - 1], f_r.at[step, d - 1], y_peer(d))

    def p_copy(piece, d):
        chunk = feature_chunk(NCHUNK - 1)
        to = lax.rem(y + d, 4)
        rows = pl.ds(piece * PIECE, PIECE)
        return remote(
            fx.at[chunk, to, rows], fin.at[y, chunk, rows], p_s.at[piece, d - 1], p_r.at[piece, d - 1], y_peer(d)
        )

    def gz_copy(d):
        return remote(gz.at[z], gz.at[z], gz_s.at[d - 1], gz_r.at[d - 1], z_peer(lax.rem(z + d, 4)))

    def gy_copy(d):
        return remote(gy.at[y], gy.at[y], gy_s.at[d - 1], gy_r.at[d - 1], y_peer(d))

    def k_copy(i):
        if i == 0:
            return remote(db.at[pl.ds((1 - core) * 4, 4)], cr, k_s.at[0], k_r.at[0], core_peer)
        part = xs.at[pl.ds(core * 4, 4)]
        return remote(part, part, k_s.at[1], k_r.at[1], core_peer)

    def x_copy(i, d):
        if i == 0:
            return remote(
                s1.at[lax.rem(x + d, 4)], xr.at[d - 1], x_s.at[0, d - 1], x_r.at[0, d - 1], x_peer(d)
            )
        part = xs.at[core * 4 + x]
        return remote(part, part, x_s.at[1, d - 1], x_r.at[1, d - 1], x_peer(d))

    def h_copy():
        return remote(zs, zr, h_s, h_r, h_peer)

    def inverse_root():
        def body(i, _):
            rows = pl.ds(pl.multiple_of(i * 16, 16), 16)
            total = jnp.zeros((16, LANE), F32)
            for j in range(D // LANE):
                v = tok_v[rows, j * LANE : (j + 1) * LANE].astype(F32)
                total = total + v * v
            mean = jnp.sum(total, axis=1, keepdims=True) / D
            rs_own[rows, :] = jnp.broadcast_to(lax.rsqrt(mean + EPSILON), (16, LANE))
            return 0

        lax.fori_loop(0, ROWS // 16, body, 0)
        rsx[y] = jnp.transpose(rs_own[...])[0:8, :]

    def spread_roots():
        def body(s, _):
            rb[s] = jnp.transpose(jnp.broadcast_to(rsx[s][0:1, :], (LANE, ROWS)))
            return 0

        lax.fori_loop(0, 4, body, 0)

    def weight_chunk(chunk):
        def norm(s, _):
            for q in range(CHUNK // LANE):
                unit = tx[chunk, s, :, q * LANE : (q + 1) * LANE].astype(F32) * rb[s]
                at = pl.multiple_of(y * BLOCK + chunk * CHUNK + q * LANE, LANE)
                normed = (unit * (1.0 + gain_v[0:1, pl.ds(at, LANE)])).astype(BF16)
                nt[s, q * LANE : (q + 1) * LANE, :] = jnp.transpose(normed)
            return 0

        lax.fori_loop(0, 4, norm, 0)

        def multiply(j, _):
            columns = pl.ds(pl.multiple_of(j * 256, 256), 256)
            total = jnp.zeros((CHUNK, 256), F32)
            for s in range(4):
                total = total + jnp.dot(nt[s], cx[s, :, columns], preferred_element_type=F32)
            gp[pl.ds(pl.multiple_of(chunk * CHUNK, CHUNK), CHUNK), columns] = total
            return 0

        lax.fori_loop(0, KW // 256, multiply, 0)

    def features(step):
        chunk = feature_chunk(step)
        product = lax.dot_general(
            cx[...].reshape(4 * ROWS, KW),
            wx[pl.ds(pl.multiple_of(chunk * CHUNK, CHUNK), CHUNK), :],
            (((1,), (1,)), ((), ())),
            preferred_element_type=F32,
        )
        fx[chunk] = product.astype(BF16).reshape(4, ROWS, CHUNK)

    def gain_part():
        gz[z] = jnp.zeros((16, LANE), F32)

        def body(t, _):
            for q in range(CHUNK // LANE):
                lanes = slice(q * LANE, (q + 1) * LANE)

                def add(s, total):
                    unit = tx[t, s, :, lanes].astype(F32) * rb[s]
                    term = fx[t, s, :, lanes].astype(F32) * unit
                    return total + jnp.sum(term.reshape(ROWS // 8, 8, LANE), axis=0)

                total = lax.fori_loop(0, 4, add, jnp.zeros((8, LANE), F32))
                gz[z, pl.ds(t * (CHUNK // LANE) + q, 1), :] = jnp.sum(total, axis=0, keepdims=True)
            return 0

        lax.fori_loop(0, NCHUNK, body, 0)

    def input_piece(piece):
        def body(i, _):
            rows = pl.ds(pl.multiple_of(piece * PIECE + i * 16, 16), 16)
            root = rs_own[rows, :]

            def terms(s, t, q):
                at = s * BLOCK + t * CHUNK + q * LANE
                grad = fin[s, t, rows, q * LANE : (q + 1) * LANE].astype(F32)
                unit = tok_v[rows, at : at + LANE].astype(F32) * root
                return at, grad * (1.0 + gain_v[0:1, at : at + LANE]), unit

            places = [(s, t, q) for s in range(4) for t in range(NCHUNK) for q in range(CHUNK // LANE)]
            total = jnp.zeros((16, LANE), F32)
            for place in places:
                _, scaled, unit = terms(*place)
                total = total + scaled * unit
            projected = jnp.sum(total, axis=1, keepdims=True) / D
            for place in places:
                at, scaled, unit = terms(*place)
                ig_v[0, rows, at : at + LANE] = (root * (scaled - unit * projected)).astype(BF16)
            return 0

        lax.fori_loop(0, PIECE // 16, body, 0)

    if WITH_FSDP:
        for i in range(4):
            start(c_copy(i))

        @pl.when(z < 3)
        def _():
            w_own(0).start()

        @pl.when(z > 0)
        def _():
            w_own(1).start()

        copies["gain"] = local(gain, gain_v, loc.at[1])
        copies["c"] = local(cotangent.at[0], cx.at[y], loc.at[2])
        copies["w"] = local(weight.at[0], wx.at[shard_rows(z)], loc.at[3])
        for step in range(NCHUNK):
            chunk = chunk_at(step)
            copies["t", step] = local(
                tokens.at[0, :, chunk_columns(y, chunk)], tx.at[chunk, y], tok_loc.at[step]
            )
    if WITH_REP:
        copies["momentum"] = local(momentum, mom_v, loc.at[5])

    if WITH_REP:
        copies["outer"].wait()
        copies["inner"].wait()
        for b in range(8):
            lanes = slice(b * LANE, (b + 1) * LANE)
            db[b] = outer_v[:, lanes] - inner_v[:, lanes].astype(F32)
        start(k_copy(0))

    if WITH_FSDP:
        copies["tokens"].wait()
        inverse_root()
        for d in (1, 3, 2):
            start(r_copy(d))
        c_copy(0).wait_recv()
        start(c_copy(4))
        c_copy(1).wait_recv()
        start(c_copy(5))
        for step in range(NCHUNK):
            for d in (1, 3, 2):
                start(t_copy(step, d))

    if WITH_REP:
        k_copy(0).wait_recv()
        for q in range(4):
            s1[q] = db[core * 4 + q] + cr[q]
        for d in (1, 2, 3):
            start(x_copy(0, d))

    if WITH_FSDP:
        weight_step(1)

    if WITH_REP:
        for d in (1, 2, 3):
            x_copy(0, d).wait_recv()
        zs[...] = (s1[x] + xr[0] + xr[1] + xr[2]).astype(BF16)
        start(h_copy())

    if WITH_FSDP:
        copies["gain"].wait()
        for d in (1, 2, 3):
            r_copy(d).wait_recv()
        spread_roots()
        copies["c"].wait()
        for i in range(2, 6):
            c_copy(i).wait_recv()
        copies["t", 0].wait()
        for d in (1, 2, 3):
            t_copy(0, d).wait_recv()
        weight_chunk(chunk_at(0))
        begin_sums(0)
        copies["w"].wait()
        weight_step(2)
        for step in range(NCHUNK - 1):
            features(step)
            for d in (1, 3, 2):
                start(f_copy(step, d))

    if WITH_REP:
        h_copy().wait_recv()
        xs[core * 4 + x] = zs[...].astype(F32) + zr[...].astype(F32)
        for d in (1, 2, 3):
            start(x_copy(1, d))

    if WITH_FSDP:
        copies["t", 1].wait()
        for d in (1, 2, 3):
            t_copy(1, d).wait_recv()
        weight_chunk(chunk_at(1))
        begin_sums(1)
        pass_sums(0, 0)

    if WITH_REP:
        for d in (1, 2, 3):
            x_copy(1, d).wait_recv()
        start(k_copy(1))

    if WITH_FSDP:
        weight_step(3)
        features(NCHUNK - 1)
        for piece in range(PIECES - 1):
            for d in (1, 3, 2):
                start(p_copy(piece, d))

    if WITH_REP:
        copies["momentum"].wait()
        k_copy(1).wait_recv()
        for b in range(8):
            lanes = slice(b * LANE, (b + 1) * LANE)
            pseudo = xs[b] / REPS
            momentum_next = MOMENTUM * mom_v[:, lanes] + pseudo
            nm_v[:, lanes] = momentum_next
            no_v[:, lanes] = outer_v[:, lanes] - OUTER_RATE * (pseudo + MOMENTUM * momentum_next)

    if WITH_FSDP:
        own = local(fx.at[:, y], fin.at[y], loc.at[7])
        pass_sums(0, 1)
        copies["t", 2].wait()
        for d in (1, 2, 3):
            t_copy(2, d).wait_recv()
        gain_part()
        for d in (1, 2, 3):
            start(gz_copy(d))
        weight_chunk(chunk_at(2))
        begin_sums(2)
        pass_sums(1, 0)
        pass_sums(2, 0)
        pass_sums(1, 1)
        for d in (1, 2, 3):
            gz_copy(d).wait_recv()
        gy[y] = gz[0] + gz[1] + gz[2] + gz[3]
        for d in (1, 3, 2):
            start(gy_copy(d))
        for d in (1, 3, 2):
            start(p_copy(PIECES - 1, d))
        pass_sums(2, 1)
        own.wait()
        for step in range(NCHUNK - 1):
            for d in (1, 2, 3):
                f_copy(step, d).wait_recv()
        for piece in range(PIECES):
            if piece == 1:
                end_sums(0)
            if piece == PIECES - 1:
                end_sums(1)
                for d in (1, 2, 3):
                    gy_copy(d).wait_recv()
                for b in range(4):
                    for i in range(BLOCK // LANE):
                        at = b * BLOCK + i * LANE
                        gg_v[0:1, at : at + LANE] = gy[b, i : i + 1, :]
            for d in (1, 2, 3):
                p_copy(piece, d).wait_recv()
            input_piece(piece)

    for copy in sends:
        copy.wait_send()
    if WITH_FSDP:

        @pl.when(z < 3)
        def _():
            w_own(0).wait_send()

        @pl.when(z > 0)
        def _():
            w_own(1).wait_send()

        for s in (1, 2):

            @pl.when((z >= s) & (z < 3))
            def _():
                w_forward(z - s, up).wait_send()

            @pl.when((z + s <= 3) & (z > 0))
            def _():
                w_forward(z + s, down).wait_send()

        for d in (1, 2, 3):
            for part in range(2):
                g_up(lax.rem(z + d, 4), part).wait_send()


def finish(*refs):
    sources, targets, sems = refs[:5], refs[5:10], refs[10]
    copies = [
        pltpu.make_async_copy(source, target, sems.at[i])
        for i, (source, target) in enumerate(zip(sources, targets))
    ]
    for copy in copies:
        copy.start()
    for copy in copies:
        copy.wait()


def call(tokens, gain, *rest):
    args = (tokens, pltpu.with_memory_space_constraint(gain, pltpu.HBM), *rest)
    shapes = (
        jax.ShapeDtypeStruct((1, ROWS, D), BF16),
        jax.ShapeDtypeStruct((1, D), F32),
        jax.ShapeDtypeStruct((1, SHARD, KW), F32),
        jax.ShapeDtypeStruct((SHARD, KW), F32),
        jax.ShapeDtypeStruct((SHARD, KW), F32),
    )
    dma = pltpu.SemaphoreType.DMA
    scratch = [
        pltpu.VMEM((ROWS, D), BF16),
        pltpu.VMEM((1, D), F32),
        pltpu.VMEM((4, ROWS, KW), BF16),
        pltpu.VMEM((BLOCK, KW), BF16),
        pltpu.VMEM((NCHUNK, 4, ROWS, CHUNK), BF16),
        pltpu.VMEM((ROWS, LANE), F32),
        pltpu.VMEM((4, 8, ROWS), F32),
        pltpu.VMEM((4, ROWS, LANE), F32),
        pltpu.VMEM((4, CHUNK, ROWS), BF16),
        pltpu.VMEM((BLOCK, KW), F32),
        pltpu.VMEM((4, SHARD, KW), BF16),
        pltpu.VMEM((4, SHARD, KW), BF16),
        pltpu.VMEM((4, SHARD, KW), BF16),
        pltpu.VMEM((NCHUNK, 4, ROWS, CHUNK), BF16),
        pltpu.VMEM((4, NCHUNK, ROWS, CHUNK), BF16),
        pltpu.VMEM((4, 16, LANE), F32),
        pltpu.VMEM((4, 16, LANE), F32),
        pltpu.VMEM((SHARD, KW), F32),
        pltpu.VMEM((SHARD, KW), F32),
        pltpu.VMEM((SHARD, KW), BF16),
        pltpu.VMEM((8, SHARD, LANE), F32),
        pltpu.VMEM((4, SHARD, LANE), F32),
        pltpu.VMEM((4, SHARD, LANE), F32),
        pltpu.VMEM((3, SHARD, LANE), F32),
        pltpu.VMEM((SHARD, LANE), BF16),
        pltpu.VMEM((SHARD, LANE), BF16),
        pltpu.VMEM((8, SHARD, LANE), F32),
        dma((8,)),
        dma((NCHUNK,)),
        dma((6,)),
        dma((6,)),
        dma((NCHUNK, 3)),
        dma((NCHUNK, 3)),
        dma((3,)),
        dma((3,)),
        dma((2,)),
        dma((4,)),
        dma((4,)),
        dma((4, 2)),
        dma((4, 2)),
        dma((4, 2)),
        dma((NCHUNK - 1, 3)),
        dma((NCHUNK - 1, 3)),
        dma((PIECES, 3)),
        dma((PIECES, 3)),
        dma((3,)),
        dma((3,)),
        dma((3,)),
        dma((3,)),
        dma((2,)),
        dma((2,)),
        dma((2, 3)),
        dma((2, 3)),
        dma,
        dma,
    ]
    anywhere = pl.BlockSpec(memory_space=pltpu.HBM)
    on_chip = pl.BlockSpec(memory_space=pltpu.VMEM)
    results = pl.pallas_call(
        kernel,
        out_shape=tuple(pltpu.VMEM(shape.shape, shape.dtype) for shape in shapes),
        in_specs=[anywhere] * 7,
        out_specs=[on_chip] * 5,
        scratch_shapes=scratch,
        compiler_params=pltpu.CompilerParams(
            collective_id=0, has_side_effects=True, vmem_limit_bytes=VMEM_LIMIT
        ),
        cost_estimate=pl.CostEstimate(
            flops=4 * ROWS * D * KW, bytes_accessed=16 * 2**20, transcendentals=ROWS
        ),
        name="inner_outer_step",
    )(*args)
    return pl.pallas_call(
        finish,
        out_shape=shapes,
        in_specs=[on_chip] * 5,
        out_specs=[anywhere] * 5,
        scratch_shapes=[pltpu.SemaphoreType.DMA((5,))],
        compiler_params=pltpu.CompilerParams(vmem_limit_bytes=2**20),
        name="write_results",
    )(*(pltpu.with_memory_space_constraint(result, pltpu.VMEM) for result in results))


def solution(mesh):
    return jax.shard_map(
        call,
        mesh=mesh,
        in_specs=(
            P("rep", "fsdp", None),
            P("rep", None),
            P("rep", "fsdp", None),
            P("rep", "fsdp", None),
            P("fsdp", None),
            P("fsdp", None),
            P("rep", "fsdp", None),
        ),
        out_specs=(
            P("rep", "fsdp", None),
            P("rep", None),
            P("rep", "fsdp", None),
            P("fsdp", None),
            P("fsdp", None),
        ),
        check_vma=False,
    )
```

```python
import jax
import jax.numpy as jnp
from jax import lax
from jax.experimental import pallas as pl
from jax.experimental.pallas import tpu as pltpu
from jax.sharding import PartitionSpec as P

EPSILON = 1e-06
OUTER_RATE = 0.7
MOMENTUM = 0.9

MESH = pl.DeviceIdType.MESH
F32 = jnp.float32
BF16 = jnp.bfloat16

D = 4608
KW = 1024
ROWS = 256
SHARD = 288
BLOCK = 1152
CHUNK = 384
NCHUNK = 3
REPS = 16
PIECES = 4
PIECE = ROWS // PIECES
HALF = ROWS // 2
PART = SHARD // 2
LANE = 128
VMEM_LIMIT = 48 * 2**20

WITH_FSDP = True
WITH_REP = True


def kernel(
    tokens,
    gain,
    weight,
    cotangent,
    outer,
    momentum,
    inner,
    ig_v,
    gg_v,
    wg_v,
    no_v,
    nm_v,
    tok_v,
    gain_v,
    cx,
    wx,
    tx,
    rs_own,
    rsx,
    rb,
    nt,
    gp,
    sb,
    ru,
    rd,
    fx,
    fin,
    gz,
    gy,
    outer_v,
    mom_v,
    inner_v,
    db,
    cr,
    s1,
    xr,
    zs,
    zr,
    xs,
    near_z,
    far_z,
    all_x,
    one_h,
    one_core,
    loc,
    tok_loc,
    c_s,
    c_r,
    t_s,
    t_r,
    r_s,
    r_r,
    w_s,
    w_f,
    w_r,
    g_s,
    u_r,
    d_r,
    f_s,
    f_r,
    p_s,
    p_r,
    gz_s,
    gz_r,
    gy_s,
    gy_r,
    k_s,
    k_r,
    x_s,
    x_r,
    h_s,
    h_r,
):
    fi = lax.axis_index("fsdp")
    ri = lax.axis_index("rep")
    y, z = fi // 4, lax.rem(fi, 4)
    x, zh, core = ri // 4, lax.rem(ri // 2, 2), lax.rem(ri, 2)

    def y_peer(d):
        return (ri, lax.rem(y + d, 4) * 4 + z)

    def z_peer(to):
        return (ri, y * 4 + to)

    def x_peer(d):
        return (lax.rem(x + d, 4) * 4 + zh * 2 + core, fi)

    h_peer = (x * 4 + (1 - zh) * 2 + core, fi)
    core_peer = (x * 4 + zh * 2 + (1 - core), fi)

    def remote(src, dst, send, recv, peer):
        return pltpu.make_async_remote_copy(
            src_ref=src, dst_ref=dst, send_sem=send, recv_sem=recv, device_id=peer, device_id_type=MESH
        )

    def local(src, dst, sem):
        copy = pltpu.make_async_copy(src, dst, sem)
        copy.start()
        return copy

    def chunk_at(step):
        return jnp.where(z < 2, NCHUNK - 1 - step, step)

    def chunk_columns(block, chunk):
        return pl.ds(pl.multiple_of(block * BLOCK + chunk * CHUNK, LANE), CHUNK)

    def shard_rows(j):
        return pl.ds(pl.multiple_of(j * SHARD, 32), SHARD)

    copies = {}
    if WITH_FSDP:
        copies["tokens"] = local(tokens.at[0], tok_v, loc.at[0])
    if WITH_REP:
        copies["outer"] = local(outer, outer_v, loc.at[4])
        copies["inner"] = local(inner.at[0], inner_v, loc.at[6])

    barrier = pltpu.get_barrier_semaphore()
    expected = 0

    def arrive(peer):
        pl.semaphore_signal(barrier, inc=1, device_id=peer, device_id_type=MESH)

    def answer(sem, peer):
        pl.semaphore_signal(sem, inc=1, device_id=peer, device_id_type=MESH)

    if WITH_FSDP:
        for d in (1, 2, 3):
            arrive(y_peer(d))
        for d in (1, 2, 3):

            @pl.when(z + d <= 3)
            def _():
                arrive(z_peer(lax.rem(z + d, 4)))

        expected = expected + 3 + z
    if WITH_REP:
        for d in (1, 2, 3):

            @pl.when(x + d <= 3)
            def _():
                arrive(x_peer(d))

        @pl.when(zh == 0)
        def _():
            arrive(h_peer)

        @pl.when(core == 1)
        def _():
            arrive(core_peer)

        expected = expected + x + zh + (1 - core)
    pl.semaphore_wait(barrier, expected)

    def answers():
        if WITH_FSDP:

            @pl.when(z >= 1)
            def _():
                answer(near_z, z_peer(jnp.maximum(z - 1, 0)))

            for d in (2, 3):

                @pl.when(z >= d)
                def _():
                    answer(far_z, z_peer(jnp.maximum(z - d, 0)))

        if WITH_REP:
            for d in (1, 2, 3):

                @pl.when(x >= d)
                def _():
                    answer(all_x, x_peer(4 - d))

            @pl.when(zh == 1)
            def _():
                answer(one_h, h_peer)

            @pl.when(core == 0)
            def _():
                answer(one_core, core_peer)

    sends = []

    def start(copy):
        copy.start()
        sends.append(copy)
        return copy

    def c_copy(i):
        first, second = pl.ds(0, HALF), pl.ds(HALF, HALF)
        if i < 4:
            rows = first if i in (0, 3) else second
            at = cx.at[y, rows]
            return remote(cotangent.at[0, rows], at, c_s.at[i], c_r.at[i], y_peer(1 if i in (0, 2) else 3))
        if i == 4:
            part = cx.at[lax.rem(y + 3, 4), first]
            return remote(part, part, c_s.at[4], c_r.at[4], y_peer(1))
        part = cx.at[lax.rem(y + 1, 4), second]
        return remote(part, part, c_s.at[5], c_r.at[5], y_peer(3))

    def t_copy(step, d):
        chunk = chunk_at(step)
        return remote(
            tokens.at[0, :, chunk_columns(lax.rem(y + d, 4), chunk)],
            tx.at[chunk, y],
            t_s.at[step, d - 1],
            t_r.at[step, d - 1],
            y_peer(d),
        )

    def r_copy(d):
        return remote(rsx.at[y], rsx.at[y], r_s.at[d - 1], r_r.at[d - 1], y_peer(d))

    up, down = jnp.minimum(z + 1, 3), jnp.maximum(z - 1, 0)

    def w_own(i):
        to = up if i == 0 else down
        return remote(weight.at[0], wx.at[shard_rows(z)], w_s.at[i], w_r.at[z], z_peer(to))

    def w_forward(j, to):
        rows = wx.at[shard_rows(j)]
        return remote(rows, rows, w_f.at[j], w_r.at[j], z_peer(to))

    def weight_step(s):
        @pl.when(z >= s)
        def _():
            w_forward(z - s, up).wait_recv()

            @pl.when(z < 3)
            def _():
                w_forward(z - s, up).start()

        @pl.when(z + s <= 3)
        def _():
            w_forward(z + s, down).wait_recv()

            @pl.when(z > 0)
            def _():
                w_forward(z + s, down).start()

    def g_up(j, part):
        at = (j, pl.ds(part * PART, PART))
        return remote(sb.at[at], ru.at[at], g_s.at[j, part], u_r.at[j, part], z_peer(up))

    def g_down(j, part):
        at = (j, pl.ds(part * PART, PART))
        return remote(sb.at[at], rd.at[at], g_s.at[j, part], d_r.at[j, part], z_peer(down))

    def send_sum(j, part, arrived, copy, first):
        def add(i, _):
            at = part * PART + i * 16
            rows = pl.ds(pl.multiple_of(at, 16), 16)
            total = gp[pl.ds(pl.multiple_of(j * SHARD + at, 16), 16), :]
            if not first:
                total = total + arrived[j, rows, :].astype(F32)
            sb[j, rows, :] = total.astype(BF16)
            return 0

        if not first:
            copy(j, part).wait_recv()
        lax.fori_loop(0, PART // 16, add, 0)
        copy(j, part).start()

    def begin_sums(step):
        @pl.when(z == 0)
        def _():
            for part in range(2):
                send_sum(3 - step, part, ru, g_up, True)

        @pl.when(z == 3)
        def _():
            for part in range(2):
                send_sum(step, part, rd, g_down, True)

    def pass_sums(step, part):
        routes = (((3, ru, g_up), (0, rd, g_down)), ((0, rd, g_down), (3, ru, g_up)), ((2, ru, g_up), (1, rd, g_down)))
        for at, (j, arrived, copy) in zip((1, 2), routes[step]):

            @pl.when(z == at)
            def _():
                send_sum(j, part, arrived, copy, False)

    def end_sums(part):
        @pl.when(z > 0)
        def _():
            g_up(z, part).wait_recv()

        @pl.when(z < 3)
        def _():
            g_down(z, part).wait_recv()

        def add(i, _):
            at = part * PART + i * 16
            rows = pl.ds(pl.multiple_of(at, 16), 16)
            wg_v[0, rows, :] = gp[pl.ds(pl.multiple_of(z * SHARD + at, 16), 16), :]

            @pl.when(z > 0)
            def _():
                wg_v[0, rows, :] += ru[z, rows, :].astype(F32)

            @pl.when(z < 3)
            def _():
                wg_v[0, rows, :] += rd[z, rows, :].astype(F32)

            return 0

        lax.fori_loop(0, PART // 16, add, 0)

    def feature_chunk(step):
        return jnp.where(z < 2, step, NCHUNK - 1 - step)

    def f_copy(step, d):
        chunk = feature_chunk(step)
        to = lax.rem(y + d, 4)
        return remote(fx.at[chunk, to], fin.at[y, chunk], f_s.at[step, d - 1], f_r.at[step, d - 1], y_peer(d))

    def p_copy(piece, d):
        chunk = feature_chunk(NCHUNK - 1)
        to = lax.rem(y + d, 4)
        rows = pl.ds(piece * PIECE, PIECE)
        return remote(
            fx.at[chunk, to, rows], fin.at[y, chunk, rows], p_s.at[piece, d - 1], p_r.at[piece, d - 1], y_peer(d)
        )

    def gz_copy(d):
        return remote(gz.at[z], gz.at[z], gz_s.at[d - 1], gz_r.at[d - 1], z_peer(lax.rem(z + d, 4)))

    def gy_copy(d):
        return remote(gy.at[y], gy.at[y], gy_s.at[d - 1], gy_r.at[d - 1], y_peer(d))

    def k_copy(i):
        if i == 0:
            return remote(db.at[pl.ds((1 - core) * 4, 4)], cr, k_s.at[0], k_r.at[0], core_peer)
        part = xs.at[pl.ds(core * 4, 4)]
        return remote(part, part, k_s.at[1], k_r.at[1], core_peer)

    def x_copy(i, d):
        if i == 0:
            return remote(
                s1.at[lax.rem(x + d, 4)], xr.at[d - 1], x_s.at[0, d - 1], x_r.at[0, d - 1], x_peer(d)
            )
        part = xs.at[core * 4 + x]
        return remote(part, part, x_s.at[1, d - 1], x_r.at[1, d - 1], x_peer(d))

    def h_copy():
        return remote(zs, zr, h_s, h_r, h_peer)

    def inverse_root():
        def body(i, _):
            rows = pl.ds(pl.multiple_of(i * 16, 16), 16)
            total = jnp.zeros((16, LANE), F32)
            for j in range(D // LANE):
                v = tok_v[rows, j * LANE : (j + 1) * LANE].astype(F32)
                total = total + v * v
            mean = jnp.sum(total, axis=1, keepdims=True) / D
            rs_own[rows, :] = jnp.broadcast_to(lax.rsqrt(mean + EPSILON), (16, LANE))
            return 0

        lax.fori_loop(0, ROWS // 16, body, 0)
        rsx[y] = jnp.transpose(rs_own[...])[0:8, :]

    def spread_roots():
        def body(s, _):
            rb[s] = jnp.transpose(jnp.broadcast_to(rsx[s][0:1, :], (LANE, ROWS)))
            return 0

        lax.fori_loop(0, 4, body, 0)

    def weight_chunk(chunk):
        def norm(s, _):
            for q in range(CHUNK // LANE):
                unit = tx[chunk, s, :, q * LANE : (q + 1) * LANE].astype(F32) * rb[s]
                at = pl.multiple_of(y * BLOCK + chunk * CHUNK + q * LANE, LANE)
                normed = (unit * (1.0 + gain_v[0:1, pl.ds(at, LANE)])).astype(BF16)
                nt[s, q * LANE : (q + 1) * LANE, :] = jnp.transpose(normed)
            return 0

        lax.fori_loop(0, 4, norm, 0)

        def multiply(j, _):
            columns = pl.ds(pl.multiple_of(j * 256, 256), 256)
            total = jnp.zeros((CHUNK, 256), F32)
            for s in range(4):
                total = total + jnp.dot(nt[s], cx[s, :, columns], preferred_element_type=F32)
            gp[pl.ds(pl.multiple_of(chunk * CHUNK, CHUNK), CHUNK), columns] = total
            return 0

        lax.fori_loop(0, KW // 256, multiply, 0)

    def features(step):
        chunk = feature_chunk(step)
        product = lax.dot_general(
            cx[...].reshape(4 * ROWS, KW),
            wx[pl.ds(pl.multiple_of(chunk * CHUNK, CHUNK), CHUNK), :],
            (((1,), (1,)), ((), ())),
            preferred_element_type=F32,
        )
        fx[chunk] = product.astype(BF16).reshape(4, ROWS, CHUNK)

    def gain_part():
        gz[z] = jnp.zeros((16, LANE), F32)

        def body(t, _):
            for q in range(CHUNK // LANE):
                lanes = slice(q * LANE, (q + 1) * LANE)

                def add(s, total):
                    unit = tx[t, s, :, lanes].astype(F32) * rb[s]
                    term = fx[t, s, :, lanes].astype(F32) * unit
                    return total + jnp.sum(term.reshape(ROWS // 8, 8, LANE), axis=0)

                total = lax.fori_loop(0, 4, add, jnp.zeros((8, LANE), F32))
                gz[z, pl.ds(t * (CHUNK // LANE) + q, 1), :] = jnp.sum(total, axis=0, keepdims=True)
            return 0

        lax.fori_loop(0, NCHUNK, body, 0)

    def input_piece(piece):
        def body(i, _):
            rows = pl.ds(pl.multiple_of(piece * PIECE + i * 16, 16), 16)
            root = rs_own[rows, :]

            def terms(s, t, q):
                at = s * BLOCK + t * CHUNK + q * LANE
                grad = fin[s, t, rows, q * LANE : (q + 1) * LANE].astype(F32)
                unit = tok_v[rows, at : at + LANE].astype(F32) * root
                return at, grad * (1.0 + gain_v[0:1, at : at + LANE]), unit

            places = [(s, t, q) for s in range(4) for t in range(NCHUNK) for q in range(CHUNK // LANE)]
            total = jnp.zeros((16, LANE), F32)
            for place in places:
                _, scaled, unit = terms(*place)
                total = total + scaled * unit
            projected = jnp.sum(total, axis=1, keepdims=True) / D
            for place in places:
                at, scaled, unit = terms(*place)
                ig_v[0, rows, at : at + LANE] = (root * (scaled - unit * projected)).astype(BF16)
            return 0

        lax.fori_loop(0, PIECE // 16, body, 0)

    if WITH_FSDP:
        for i in range(4):
            start(c_copy(i))

        @pl.when(z > 0)
        def _():
            w_own(1).start()

        answers()

        copies["gain"] = local(gain, gain_v, loc.at[1])
        copies["c"] = local(cotangent.at[0], cx.at[y], loc.at[2])
        copies["w"] = local(weight.at[0], wx.at[shard_rows(z)], loc.at[3])
        for step in range(NCHUNK):
            chunk = chunk_at(step)
            copies["t", step] = local(
                tokens.at[0, :, chunk_columns(y, chunk)], tx.at[chunk, y], tok_loc.at[step]
            )
    if WITH_REP:
        copies["momentum"] = local(momentum, mom_v, loc.at[5])
    if not WITH_FSDP:
        answers()
    if WITH_FSDP:

        @pl.when(z < 3)
        def _():
            pl.semaphore_wait(near_z, 1)
            w_own(0).start()

    if WITH_REP:
        copies["outer"].wait()
        copies["inner"].wait()
        for b in range(8):
            lanes = slice(b * LANE, (b + 1) * LANE)
            db[b] = outer_v[:, lanes] - inner_v[:, lanes].astype(F32)

        @pl.when(core == 1)
        def _():
            pl.semaphore_wait(one_core, 1)

        start(k_copy(0))

    if WITH_FSDP:
        copies["tokens"].wait()
        inverse_root()
        for d in (1, 3, 2):
            start(r_copy(d))
        c_copy(0).wait_recv()
        start(c_copy(4))
        c_copy(1).wait_recv()
        start(c_copy(5))
        for step in range(NCHUNK):
            for d in (1, 3, 2):
                start(t_copy(step, d))

    if WITH_REP:
        k_copy(0).wait_recv()
        for q in range(4):
            s1[q] = db[core * 4 + q] + cr[q]

        @pl.when(x < 3)
        def _():
            pl.semaphore_wait(all_x, 3 - x)

        for d in (1, 2, 3):
            start(x_copy(0, d))

    if WITH_FSDP:
        weight_step(1)

    if WITH_REP:
        for d in (1, 2, 3):
            x_copy(0, d).wait_recv()
        zs[...] = (s1[x] + xr[0] + xr[1] + xr[2]).astype(BF16)

        @pl.when(zh == 0)
        def _():
            pl.semaphore_wait(one_h, 1)

        start(h_copy())

    if WITH_FSDP:
        copies["gain"].wait()
        for d in (1, 2, 3):
            r_copy(d).wait_recv()
        spread_roots()
        copies["c"].wait()
        for i in range(2, 6):
            c_copy(i).wait_recv()
        copies["t", 0].wait()
        for d in (1, 2, 3):
            t_copy(0, d).wait_recv()
        weight_chunk(chunk_at(0))
        begin_sums(0)
        copies["w"].wait()
        weight_step(2)
        for step in range(NCHUNK - 1):
            features(step)
            for d in (1, 3, 2):
                start(f_copy(step, d))

    if WITH_REP:
        h_copy().wait_recv()
        xs[core * 4 + x] = zs[...].astype(F32) + zr[...].astype(F32)
        for d in (1, 2, 3):
            start(x_copy(1, d))

    if WITH_FSDP:
        copies["t", 1].wait()
        for d in (1, 2, 3):
            t_copy(1, d).wait_recv()
        weight_chunk(chunk_at(1))
        begin_sums(1)
        pass_sums(0, 0)

    if WITH_REP:
        for d in (1, 2, 3):
            x_copy(1, d).wait_recv()
        start(k_copy(1))

    if WITH_FSDP:
        weight_step(3)
        features(NCHUNK - 1)
        for piece in range(PIECES - 1):
            for d in (1, 3, 2):
                start(p_copy(piece, d))

    if WITH_REP:
        copies["momentum"].wait()
        k_copy(1).wait_recv()
        for b in range(8):
            lanes = slice(b * LANE, (b + 1) * LANE)
            pseudo = xs[b] / REPS
            momentum_next = MOMENTUM * mom_v[:, lanes] + pseudo
            nm_v[:, lanes] = momentum_next
            no_v[:, lanes] = outer_v[:, lanes] - OUTER_RATE * (pseudo + MOMENTUM * momentum_next)

    if WITH_FSDP:
        own = local(fx.at[:, y], fin.at[y], loc.at[7])
        pass_sums(0, 1)
        copies["t", 2].wait()
        for d in (1, 2, 3):
            t_copy(2, d).wait_recv()
        gain_part()

        @pl.when(z < 2)
        def _():
            pl.semaphore_wait(far_z, 2 - z)

        for d in (1, 2, 3):
            start(gz_copy(d))
        weight_chunk(chunk_at(2))
        begin_sums(2)
        pass_sums(1, 0)
        pass_sums(2, 0)
        pass_sums(1, 1)
        for d in (1, 2, 3):
            gz_copy(d).wait_recv()
        gy[y] = gz[0] + gz[1] + gz[2] + gz[3]
        for d in (1, 3, 2):
            start(gy_copy(d))
        for d in (1, 3, 2):
            start(p_copy(PIECES - 1, d))
        pass_sums(2, 1)
        own.wait()
        for step in range(NCHUNK - 1):
            for d in (1, 2, 3):
                f_copy(step, d).wait_recv()
        for piece in range(PIECES):
            if piece == 1:
                end_sums(0)
            if piece == PIECES - 1:
                end_sums(1)
                for d in (1, 2, 3):
                    gy_copy(d).wait_recv()
                for b in range(4):
                    for i in range(BLOCK // LANE):
                        at = b * BLOCK + i * LANE
                        gg_v[0:1, at : at + LANE] = gy[b, i : i + 1, :]
            for d in (1, 2, 3):
                p_copy(piece, d).wait_recv()
            input_piece(piece)

    for copy in sends:
        copy.wait_send()
    if WITH_FSDP:

        @pl.when(z < 3)
        def _():
            w_own(0).wait_send()

        @pl.when(z > 0)
        def _():
            w_own(1).wait_send()

        for s in (1, 2):

            @pl.when((z >= s) & (z < 3))
            def _():
                w_forward(z - s, up).wait_send()

            @pl.when((z + s <= 3) & (z > 0))
            def _():
                w_forward(z + s, down).wait_send()

        for d in (1, 2, 3):
            for part in range(2):
                g_up(lax.rem(z + d, 4), part).wait_send()


def finish(*refs):
    sources, targets, sems = refs[:5], refs[5:10], refs[10]
    copies = [
        pltpu.make_async_copy(source, target, sems.at[i])
        for i, (source, target) in enumerate(zip(sources, targets))
    ]
    for copy in copies:
        copy.start()
    for copy in copies:
        copy.wait()


def call(tokens, gain, *rest):
    args = (tokens, pltpu.with_memory_space_constraint(gain, pltpu.HBM), *rest)
    shapes = (
        jax.ShapeDtypeStruct((1, ROWS, D), BF16),
        jax.ShapeDtypeStruct((1, D), F32),
        jax.ShapeDtypeStruct((1, SHARD, KW), F32),
        jax.ShapeDtypeStruct((SHARD, KW), F32),
        jax.ShapeDtypeStruct((SHARD, KW), F32),
    )
    dma = pltpu.SemaphoreType.DMA
    scratch = [
        pltpu.VMEM((ROWS, D), BF16),
        pltpu.VMEM((1, D), F32),
        pltpu.VMEM((4, ROWS, KW), BF16),
        pltpu.VMEM((BLOCK, KW), BF16),
        pltpu.VMEM((NCHUNK, 4, ROWS, CHUNK), BF16),
        pltpu.VMEM((ROWS, LANE), F32),
        pltpu.VMEM((4, 8, ROWS), F32),
        pltpu.VMEM((4, ROWS, LANE), F32),
        pltpu.VMEM((4, CHUNK, ROWS), BF16),
        pltpu.VMEM((BLOCK, KW), F32),
        pltpu.VMEM((4, SHARD, KW), BF16),
        pltpu.VMEM((4, SHARD, KW), BF16),
        pltpu.VMEM((4, SHARD, KW), BF16),
        pltpu.VMEM((NCHUNK, 4, ROWS, CHUNK), BF16),
        pltpu.VMEM((4, NCHUNK, ROWS, CHUNK), BF16),
        pltpu.VMEM((4, 16, LANE), F32),
        pltpu.VMEM((4, 16, LANE), F32),
        pltpu.VMEM((SHARD, KW), F32),
        pltpu.VMEM((SHARD, KW), F32),
        pltpu.VMEM((SHARD, KW), BF16),
        pltpu.VMEM((8, SHARD, LANE), F32),
        pltpu.VMEM((4, SHARD, LANE), F32),
        pltpu.VMEM((4, SHARD, LANE), F32),
        pltpu.VMEM((3, SHARD, LANE), F32),
        pltpu.VMEM((SHARD, LANE), BF16),
        pltpu.VMEM((SHARD, LANE), BF16),
        pltpu.VMEM((8, SHARD, LANE), F32),
        pltpu.SemaphoreType.REGULAR,
        pltpu.SemaphoreType.REGULAR,
        pltpu.SemaphoreType.REGULAR,
        pltpu.SemaphoreType.REGULAR,
        pltpu.SemaphoreType.REGULAR,
        dma((8,)),
        dma((NCHUNK,)),
        dma((6,)),
        dma((6,)),
        dma((NCHUNK, 3)),
        dma((NCHUNK, 3)),
        dma((3,)),
        dma((3,)),
        dma((2,)),
        dma((4,)),
        dma((4,)),
        dma((4, 2)),
        dma((4, 2)),
        dma((4, 2)),
        dma((NCHUNK - 1, 3)),
        dma((NCHUNK - 1, 3)),
        dma((PIECES, 3)),
        dma((PIECES, 3)),
        dma((3,)),
        dma((3,)),
        dma((3,)),
        dma((3,)),
        dma((2,)),
        dma((2,)),
        dma((2, 3)),
        dma((2, 3)),
        dma,
        dma,
    ]
    anywhere = pl.BlockSpec(memory_space=pltpu.HBM)
    on_chip = pl.BlockSpec(memory_space=pltpu.VMEM)
    results = pl.pallas_call(
        kernel,
        out_shape=tuple(pltpu.VMEM(shape.shape, shape.dtype) for shape in shapes),
        in_specs=[anywhere] * 7,
        out_specs=[on_chip] * 5,
        scratch_shapes=scratch,
        compiler_params=pltpu.CompilerParams(
            collective_id=0, has_side_effects=True, vmem_limit_bytes=VMEM_LIMIT
        ),
        cost_estimate=pl.CostEstimate(
            flops=4 * ROWS * D * KW, bytes_accessed=16 * 2**20, transcendentals=ROWS
        ),
        name="inner_outer_step",
    )(*args)
    return pl.pallas_call(
        finish,
        out_shape=shapes,
        in_specs=[on_chip] * 5,
        out_specs=[anywhere] * 5,
        scratch_shapes=[pltpu.SemaphoreType.DMA((5,))],
        compiler_params=pltpu.CompilerParams(vmem_limit_bytes=2**20),
        name="write_results",
    )(*(pltpu.with_memory_space_constraint(result, pltpu.VMEM) for result in results))


def solution(mesh):
    return jax.shard_map(
        call,
        mesh=mesh,
        in_specs=(
            P("rep", "fsdp", None),
            P("rep", None),
            P("rep", "fsdp", None),
            P("rep", "fsdp", None),
            P("fsdp", None),
            P("fsdp", None),
            P("rep", "fsdp", None),
        ),
        out_specs=(
            P("rep", "fsdp", None),
            P("rep", None),
            P("rep", "fsdp", None),
            P("fsdp", None),
            P("fsdp", None),
        ),
        check_vma=False,
    )
```

```python
import jax
import jax.numpy as jnp
from jax import lax
from jax.experimental import pallas as pl
from jax.experimental.pallas import tpu as pltpu
from jax.sharding import PartitionSpec as P

EPSILON = 1e-06
OUTER_RATE = 0.7
MOMENTUM = 0.9

MESH = pl.DeviceIdType.MESH
F32 = jnp.float32
BF16 = jnp.bfloat16

D = 4608
KW = 1024
ROWS = 256
SHARD = 288
BLOCK = 1152
CHUNK = 384
NCHUNK = 3
REPS = 16
PIECES = 8
PIECE = ROWS // PIECES
HALF = ROWS // 2
PART = SHARD // 2
LANE = 128
VMEM_LIMIT = 48 * 2**20

WITH_FSDP = True
WITH_REP = True


def kernel(
    tokens,
    gain,
    weight,
    cotangent,
    outer,
    momentum,
    inner,
    ig_v,
    gg_v,
    wg_v,
    no_v,
    nm_v,
    tok_v,
    gain_v,
    cx,
    wx,
    tx,
    rs_own,
    rsx,
    rb,
    nt,
    gp,
    sb,
    ru,
    rd,
    fx,
    fin,
    gz,
    gy,
    outer_v,
    mom_v,
    inner_v,
    db,
    cr,
    s1,
    xr,
    zs,
    zr,
    xs,
    near_z,
    far_z,
    all_x,
    one_h,
    one_core,
    loc,
    tok_loc,
    c_s,
    c_r,
    t_s,
    t_r,
    r_s,
    r_r,
    w_s,
    w_f,
    w_r,
    g_s,
    u_r,
    d_r,
    f_s,
    f_r,
    p_s,
    p_r,
    gz_s,
    gz_r,
    gy_s,
    gy_r,
    k_s,
    k_r,
    x_s,
    x_r,
    h_s,
    h_r,
):
    fi = lax.axis_index("fsdp")
    ri = lax.axis_index("rep")
    y, z = fi // 4, lax.rem(fi, 4)
    x, zh, core = ri // 4, lax.rem(ri // 2, 2), lax.rem(ri, 2)

    def y_peer(d):
        return (ri, lax.rem(y + d, 4) * 4 + z)

    def z_peer(to):
        return (ri, y * 4 + to)

    def x_peer(d):
        return (lax.rem(x + d, 4) * 4 + zh * 2 + core, fi)

    h_peer = (x * 4 + (1 - zh) * 2 + core, fi)
    core_peer = (x * 4 + zh * 2 + (1 - core), fi)

    def remote(src, dst, send, recv, peer):
        return pltpu.make_async_remote_copy(
            src_ref=src, dst_ref=dst, send_sem=send, recv_sem=recv, device_id=peer, device_id_type=MESH
        )

    def local(src, dst, sem):
        copy = pltpu.make_async_copy(src, dst, sem)
        copy.start()
        return copy

    def chunk_at(step):
        return jnp.where(z < 2, NCHUNK - 1 - step, step)

    def chunk_columns(block, chunk):
        return pl.ds(pl.multiple_of(block * BLOCK + chunk * CHUNK, LANE), CHUNK)

    def shard_rows(j):
        return pl.ds(pl.multiple_of(j * SHARD, 32), SHARD)

    barrier = pltpu.get_barrier_semaphore()
    expected = 0

    def arrive(peer):
        pl.semaphore_signal(barrier, inc=1, device_id=peer, device_id_type=MESH)

    def answer(sem, peer):
        pl.semaphore_signal(sem, inc=1, device_id=peer, device_id_type=MESH)

    if WITH_FSDP:
        for d in (1, 2, 3):
            arrive(y_peer(d))
        for d in (1, 2, 3):

            @pl.when(z + d <= 3)
            def _():
                arrive(z_peer(lax.rem(z + d, 4)))

        expected = expected + 3 + z
    if WITH_REP:
        for d in (1, 2, 3):

            @pl.when(x + d <= 3)
            def _():
                arrive(x_peer(d))

        @pl.when(zh == 0)
        def _():
            arrive(h_peer)

        @pl.when(core == 1)
        def _():
            arrive(core_peer)

        expected = expected + x + zh + (1 - core)
    copies = {}
    if WITH_FSDP:
        copies["tokens"] = local(tokens.at[0], tok_v, loc.at[0])
    if WITH_REP:
        copies["outer"] = local(outer, outer_v, loc.at[4])
        copies["inner"] = local(inner.at[0], inner_v, loc.at[6])

    pl.semaphore_wait(barrier, expected)

    def answers():
        if WITH_FSDP:

            @pl.when(z >= 1)
            def _():
                answer(near_z, z_peer(jnp.maximum(z - 1, 0)))

            for d in (2, 3):

                @pl.when(z >= d)
                def _():
                    answer(far_z, z_peer(jnp.maximum(z - d, 0)))

        if WITH_REP:
            for d in (1, 2, 3):

                @pl.when(x >= d)
                def _():
                    answer(all_x, x_peer(4 - d))

            @pl.when(zh == 1)
            def _():
                answer(one_h, h_peer)

            @pl.when(core == 0)
            def _():
                answer(one_core, core_peer)

    sends = []

    def start(copy):
        copy.start()
        sends.append(copy)
        return copy

    def c_copy(i):
        first, second = pl.ds(0, HALF), pl.ds(HALF, HALF)
        if i < 4:
            rows = first if i in (0, 3) else second
            at = cx.at[y, rows]
            return remote(cotangent.at[0, rows], at, c_s.at[i], c_r.at[i], y_peer(1 if i in (0, 2) else 3))
        if i == 4:
            part = cx.at[lax.rem(y + 3, 4), first]
            return remote(part, part, c_s.at[4], c_r.at[4], y_peer(1))
        part = cx.at[lax.rem(y + 1, 4), second]
        return remote(part, part, c_s.at[5], c_r.at[5], y_peer(3))

    def t_copy(step, d):
        chunk = chunk_at(step)
        return remote(
            tokens.at[0, :, chunk_columns(lax.rem(y + d, 4), chunk)],
            tx.at[chunk, y],
            t_s.at[step, d - 1],
            t_r.at[step, d - 1],
            y_peer(d),
        )

    def r_copy(d):
        return remote(rsx.at[y], rsx.at[y], r_s.at[d - 1], r_r.at[d - 1], y_peer(d))

    up, down = jnp.minimum(z + 1, 3), jnp.maximum(z - 1, 0)

    def w_own(i):
        to = up if i == 0 else down
        return remote(weight.at[0], wx.at[shard_rows(z)], w_s.at[i], w_r.at[z], z_peer(to))

    def w_forward(j, to):
        rows = wx.at[shard_rows(j)]
        return remote(rows, rows, w_f.at[j], w_r.at[j], z_peer(to))

    def weight_step(s):
        @pl.when(z >= s)
        def _():
            w_forward(z - s, up).wait_recv()

            @pl.when(z < 3)
            def _():
                w_forward(z - s, up).start()

        @pl.when(z + s <= 3)
        def _():
            w_forward(z + s, down).wait_recv()

            @pl.when(z > 0)
            def _():
                w_forward(z + s, down).start()

    def g_up(j, part):
        at = (j, pl.ds(part * PART, PART))
        return remote(sb.at[at], ru.at[at], g_s.at[j, part], u_r.at[j, part], z_peer(up))

    def g_down(j, part):
        at = (j, pl.ds(part * PART, PART))
        return remote(sb.at[at], rd.at[at], g_s.at[j, part], d_r.at[j, part], z_peer(down))

    def send_sum(j, part, arrived, copy, first):
        def add(i, _):
            at = part * PART + i * 16
            rows = pl.ds(pl.multiple_of(at, 16), 16)
            total = gp[pl.ds(pl.multiple_of(j * SHARD + at, 16), 16), :]
            if not first:
                total = total + arrived[j, rows, :].astype(F32)
            sb[j, rows, :] = total.astype(BF16)
            return 0

        if not first:
            copy(j, part).wait_recv()
        lax.fori_loop(0, PART // 16, add, 0)
        copy(j, part).start()

    def begin_sums(step):
        @pl.when(z == 0)
        def _():
            for part in range(2):
                send_sum(3 - step, part, ru, g_up, True)

        @pl.when(z == 3)
        def _():
            for part in range(2):
                send_sum(step, part, rd, g_down, True)

    def pass_sums(step, part):
        routes = (((3, ru, g_up), (0, rd, g_down)), ((0, rd, g_down), (3, ru, g_up)), ((2, ru, g_up), (1, rd, g_down)))
        for at, (j, arrived, copy) in zip((1, 2), routes[step]):

            @pl.when(z == at)
            def _():
                send_sum(j, part, arrived, copy, False)

    def end_sums(part):
        @pl.when(z > 0)
        def _():
            g_up(z, part).wait_recv()

        @pl.when(z < 3)
        def _():
            g_down(z, part).wait_recv()

        def add(i, _):
            at = part * PART + i * 16
            rows = pl.ds(pl.multiple_of(at, 16), 16)
            wg_v[0, rows, :] = gp[pl.ds(pl.multiple_of(z * SHARD + at, 16), 16), :]

            @pl.when(z > 0)
            def _():
                wg_v[0, rows, :] += ru[z, rows, :].astype(F32)

            @pl.when(z < 3)
            def _():
                wg_v[0, rows, :] += rd[z, rows, :].astype(F32)

            return 0

        lax.fori_loop(0, PART // 16, add, 0)

    def feature_chunk(step):
        return jnp.where(z < 2, step, NCHUNK - 1 - step)

    def f_copy(step, d):
        chunk = feature_chunk(step)
        to = lax.rem(y + d, 4)
        return remote(fx.at[chunk, to], fin.at[y, chunk], f_s.at[step, d - 1], f_r.at[step, d - 1], y_peer(d))

    def p_copy(piece, d):
        chunk = feature_chunk(NCHUNK - 1)
        to = lax.rem(y + d, 4)
        rows = pl.ds(pl.multiple_of(piece * PIECE, 16), PIECE)
        return remote(
            fx.at[chunk, to, rows], fin.at[y, chunk, rows], p_s.at[piece, d - 1], p_r.at[piece, d - 1], y_peer(d)
        )

    def gz_copy(d):
        return remote(gz.at[z], gz.at[z], gz_s.at[d - 1], gz_r.at[d - 1], z_peer(lax.rem(z + d, 4)))

    def gy_copy(d):
        return remote(gy.at[y], gy.at[y], gy_s.at[d - 1], gy_r.at[d - 1], y_peer(d))

    def k_copy(i):
        if i == 0:
            return remote(db.at[pl.ds((1 - core) * 4, 4)], cr, k_s.at[0], k_r.at[0], core_peer)
        part = xs.at[pl.ds(core * 4, 4)]
        return remote(part, part, k_s.at[1], k_r.at[1], core_peer)

    def x_copy(i, d):
        if i == 0:
            return remote(
                s1.at[lax.rem(x + d, 4)], xr.at[d - 1], x_s.at[0, d - 1], x_r.at[0, d - 1], x_peer(d)
            )
        part = xs.at[core * 4 + x]
        return remote(part, part, x_s.at[1, d - 1], x_r.at[1, d - 1], x_peer(d))

    def h_copy():
        return remote(zs, zr, h_s, h_r, h_peer)

    def inverse_root():
        def body(i, _):
            rows = pl.ds(pl.multiple_of(i * 16, 16), 16)
            total = jnp.zeros((16, LANE), F32)
            for j in range(D // LANE):
                v = tok_v[rows, j * LANE : (j + 1) * LANE].astype(F32)
                total = total + v * v
            mean = jnp.sum(total, axis=1, keepdims=True) / D
            rs_own[rows, :] = jnp.broadcast_to(lax.rsqrt(mean + EPSILON), (16, LANE))
            return 0

        lax.fori_loop(0, ROWS // 16, body, 0)
        rsx[y] = jnp.transpose(rs_own[...])[0:8, :]

    def spread_roots():
        def body(s, _):
            rb[s] = jnp.transpose(jnp.broadcast_to(rsx[s][0:1, :], (LANE, ROWS)))
            return 0

        lax.fori_loop(0, 4, body, 0)

    def weight_chunk(chunk):
        def norm(s, _):
            for q in range(CHUNK // LANE):
                unit = tx[chunk, s, :, q * LANE : (q + 1) * LANE].astype(F32) * rb[s]
                at = pl.multiple_of(y * BLOCK + chunk * CHUNK + q * LANE, LANE)
                normed = (unit * (1.0 + gain_v[0:1, pl.ds(at, LANE)])).astype(BF16)
                nt[s, q * LANE : (q + 1) * LANE, :] = jnp.transpose(normed)
            return 0

        lax.fori_loop(0, 4, norm, 0)

        def multiply(j, _):
            columns = pl.ds(pl.multiple_of(j * 256, 256), 256)
            total = jnp.zeros((CHUNK, 256), F32)
            for s in range(4):
                total = total + jnp.dot(nt[s], cx[s, :, columns], preferred_element_type=F32)
            gp[pl.ds(pl.multiple_of(chunk * CHUNK, CHUNK), CHUNK), columns] = total
            return 0

        lax.fori_loop(0, KW // 256, multiply, 0)

    def features(step):
        chunk = feature_chunk(step)
        rows = pl.ds(pl.multiple_of(chunk * CHUNK, CHUNK), CHUNK)

        def body(s, _):
            product = lax.dot_general(cx[s], wx[rows, :], (((1,), (1,)), ((), ())), preferred_element_type=F32)
            fx[chunk, s] = product.astype(BF16)
            return 0

        lax.fori_loop(0, 4, body, 0)

    def gain_part():
        gz[z] = jnp.zeros((16, LANE), F32)

        def body(t, _):
            for q in range(CHUNK // LANE):
                lanes = slice(q * LANE, (q + 1) * LANE)

                def add(s, total):
                    unit = tx[t, s, :, lanes].astype(F32) * rb[s]
                    term = fx[t, s, :, lanes].astype(F32) * unit
                    return total + jnp.sum(term.reshape(ROWS // 8, 8, LANE), axis=0)

                total = lax.fori_loop(0, 4, add, jnp.zeros((8, LANE), F32))
                gz[z, pl.ds(t * (CHUNK // LANE) + q, 1), :] = jnp.sum(total, axis=0, keepdims=True)
            return 0

        lax.fori_loop(0, NCHUNK, body, 0)

    def input_piece(piece):
        def body(i, _):
            rows = pl.ds(pl.multiple_of(piece * PIECE + i * 16, 16), 16)
            root = rs_own[rows, :]

            def terms(s, t, q):
                at = s * BLOCK + t * CHUNK + q * LANE
                grad = fin[s, t, rows, q * LANE : (q + 1) * LANE].astype(F32)
                unit = tok_v[rows, at : at + LANE].astype(F32) * root
                return at, grad * (1.0 + gain_v[0:1, at : at + LANE]), unit

            places = [(s, t, q) for s in range(4) for t in range(NCHUNK) for q in range(CHUNK // LANE)]
            total = jnp.zeros((16, LANE), F32)
            for place in places:
                _, scaled, unit = terms(*place)
                total = total + scaled * unit
            projected = jnp.sum(total, axis=1, keepdims=True) / D
            for place in places:
                at, scaled, unit = terms(*place)
                ig_v[0, rows, at : at + LANE] = (root * (scaled - unit * projected)).astype(BF16)
            return 0

        lax.fori_loop(0, PIECE // 16, body, 0)

    if WITH_FSDP:
        for i in range(4):
            start(c_copy(i))

        @pl.when(z > 0)
        def _():
            w_own(1).start()

        for d in (1, 3, 2):
            start(t_copy(0, d))

        answers()

        copies["gain"] = local(gain, gain_v, loc.at[1])
        copies["c"] = local(cotangent.at[0], cx.at[y], loc.at[2])
        copies["w"] = local(weight.at[0], wx.at[shard_rows(z)], loc.at[3])
        for step in range(NCHUNK):
            chunk = chunk_at(step)
            copies["t", step] = local(
                tokens.at[0, :, chunk_columns(y, chunk)], tx.at[chunk, y], tok_loc.at[step]
            )
    if WITH_REP:
        copies["momentum"] = local(momentum, mom_v, loc.at[5])
    if not WITH_FSDP:
        answers()
    if WITH_FSDP:

        @pl.when(z < 3)
        def _():
            pl.semaphore_wait(near_z, 1)
            w_own(0).start()

    if WITH_REP:
        copies["outer"].wait()
        copies["inner"].wait()

        def differ(b, _):
            lanes = pl.ds(pl.multiple_of(b * LANE, LANE), LANE)
            db[b] = outer_v[:, lanes] - inner_v[:, lanes].astype(F32)
            return 0

        lax.fori_loop(0, 8, differ, 0)

        @pl.when(core == 1)
        def _():
            pl.semaphore_wait(one_core, 1)

        start(k_copy(0))

    if WITH_FSDP:
        copies["tokens"].wait()
        inverse_root()
        for d in (1, 3, 2):
            start(r_copy(d))
        c_copy(0).wait_recv()
        start(c_copy(4))
        c_copy(1).wait_recv()
        start(c_copy(5))
        for step in range(1, NCHUNK):
            for d in (1, 3, 2):
                start(t_copy(step, d))

    if WITH_REP:
        k_copy(0).wait_recv()
        for q in range(4):
            s1[q] = db[core * 4 + q] + cr[q]

        @pl.when(x < 3)
        def _():
            pl.semaphore_wait(all_x, 3 - x)

        for d in (1, 2, 3):
            start(x_copy(0, d))

    if WITH_FSDP:
        weight_step(1)

    if WITH_REP:
        for d in (1, 2, 3):
            x_copy(0, d).wait_recv()
        zs[...] = (s1[x] + xr[0] + xr[1] + xr[2]).astype(BF16)

        @pl.when(zh == 0)
        def _():
            pl.semaphore_wait(one_h, 1)

        start(h_copy())

    if WITH_FSDP:
        copies["gain"].wait()
        for d in (1, 2, 3):
            r_copy(d).wait_recv()
        spread_roots()
        copies["c"].wait()
        for i in range(2, 6):
            c_copy(i).wait_recv()
        copies["t", 0].wait()
        for d in (1, 2, 3):
            t_copy(0, d).wait_recv()
        weight_chunk(chunk_at(0))
        begin_sums(0)
        copies["w"].wait()
        weight_step(2)

        def early_features(step, _):
            features(step)
            for d in (1, 3, 2):
                f_copy(step, d).start()
            return 0

        lax.fori_loop(0, NCHUNK - 1, early_features, 0)

    if WITH_REP:
        h_copy().wait_recv()
        xs[core * 4 + x] = zs[...].astype(F32) + zr[...].astype(F32)
        for d in (1, 2, 3):
            start(x_copy(1, d))

    if WITH_FSDP:
        copies["t", 1].wait()
        for d in (1, 2, 3):
            t_copy(1, d).wait_recv()
        weight_chunk(chunk_at(1))
        begin_sums(1)
        pass_sums(0, 0)

    if WITH_REP:
        for d in (1, 2, 3):
            x_copy(1, d).wait_recv()
        start(k_copy(1))

    if WITH_FSDP:
        weight_step(3)
        features(NCHUNK - 1)
        for piece in range(PIECES):
            for d in (1, 3, 2):
                start(p_copy(piece, d))

    if WITH_REP:
        copies["momentum"].wait()
        k_copy(1).wait_recv()

        def nesterov(b, _):
            lanes = pl.ds(pl.multiple_of(b * LANE, LANE), LANE)
            pseudo = xs[b] / REPS
            momentum_next = MOMENTUM * mom_v[:, lanes] + pseudo
            nm_v[:, lanes] = momentum_next
            no_v[:, lanes] = outer_v[:, lanes] - OUTER_RATE * (pseudo + MOMENTUM * momentum_next)
            return 0

        lax.fori_loop(0, 8, nesterov, 0)

    if WITH_FSDP:
        own = local(fx.at[:, y], fin.at[y], loc.at[7])
        pass_sums(0, 1)
        copies["t", 2].wait()
        for d in (1, 2, 3):
            t_copy(2, d).wait_recv()
        gain_part()

        @pl.when(z < 2)
        def _():
            pl.semaphore_wait(far_z, 2 - z)

        for d in (1, 2, 3):
            start(gz_copy(d))
        weight_chunk(chunk_at(2))
        begin_sums(2)
        pass_sums(1, 0)
        pass_sums(2, 0)
        pass_sums(1, 1)
        for d in (1, 2, 3):
            gz_copy(d).wait_recv()
        gy[y] = gz[0] + gz[1] + gz[2] + gz[3]
        for d in (1, 3, 2):
            start(gy_copy(d))
        pass_sums(2, 1)
        own.wait()
        for step in range(NCHUNK - 1):
            for d in (1, 2, 3):
                f_copy(step, d).wait_recv()

        def last_rows(piece, _):
            for d in (1, 2, 3):
                p_copy(piece, d).wait_recv()
            input_piece(piece)
            return 0

        end_sums(0)
        lax.fori_loop(0, PIECES, last_rows, 0)
        end_sums(1)
        for d in (1, 2, 3):
            gy_copy(d).wait_recv()
        for b in range(4):
            for i in range(BLOCK // LANE):
                at = b * BLOCK + i * LANE
                gg_v[0:1, at : at + LANE] = gy[b, i : i + 1, :]

    for copy in sends:
        copy.wait_send()
    if WITH_FSDP:
        for step in range(NCHUNK - 1):
            for d in (1, 2, 3):
                f_copy(step, d).wait_send()

        @pl.when(z < 3)
        def _():
            w_own(0).wait_send()

        @pl.when(z > 0)
        def _():
            w_own(1).wait_send()

        for s in (1, 2):

            @pl.when((z >= s) & (z < 3))
            def _():
                w_forward(z - s, up).wait_send()

            @pl.when((z + s <= 3) & (z > 0))
            def _():
                w_forward(z + s, down).wait_send()

        for d in (1, 2, 3):
            for part in range(2):
                g_up(lax.rem(z + d, 4), part).wait_send()


def finish(*refs):
    sources, targets, sems = refs[:5], refs[5:10], refs[10]
    copies = [
        pltpu.make_async_copy(source, target, sems.at[i])
        for i, (source, target) in enumerate(zip(sources, targets))
    ]
    for copy in copies:
        copy.start()
    for copy in copies:
        copy.wait()


def call(tokens, gain, *rest):
    args = (tokens, pltpu.with_memory_space_constraint(gain, pltpu.HBM), *rest)
    shapes = (
        jax.ShapeDtypeStruct((1, ROWS, D), BF16),
        jax.ShapeDtypeStruct((1, D), F32),
        jax.ShapeDtypeStruct((1, SHARD, KW), F32),
        jax.ShapeDtypeStruct((SHARD, KW), F32),
        jax.ShapeDtypeStruct((SHARD, KW), F32),
    )
    dma = pltpu.SemaphoreType.DMA
    scratch = [
        pltpu.VMEM((ROWS, D), BF16),
        pltpu.VMEM((1, D), F32),
        pltpu.VMEM((4, ROWS, KW), BF16),
        pltpu.VMEM((BLOCK, KW), BF16),
        pltpu.VMEM((NCHUNK, 4, ROWS, CHUNK), BF16),
        pltpu.VMEM((ROWS, LANE), F32),
        pltpu.VMEM((4, 8, ROWS), F32),
        pltpu.VMEM((4, ROWS, LANE), F32),
        pltpu.VMEM((4, CHUNK, ROWS), BF16),
        pltpu.VMEM((BLOCK, KW), F32),
        pltpu.VMEM((4, SHARD, KW), BF16),
        pltpu.VMEM((4, SHARD, KW), BF16),
        pltpu.VMEM((4, SHARD, KW), BF16),
        pltpu.VMEM((NCHUNK, 4, ROWS, CHUNK), BF16),
        pltpu.VMEM((4, NCHUNK, ROWS, CHUNK), BF16),
        pltpu.VMEM((4, 16, LANE), F32),
        pltpu.VMEM((4, 16, LANE), F32),
        pltpu.VMEM((SHARD, KW), F32),
        pltpu.VMEM((SHARD, KW), F32),
        pltpu.VMEM((SHARD, KW), BF16),
        pltpu.VMEM((8, SHARD, LANE), F32),
        pltpu.VMEM((4, SHARD, LANE), F32),
        pltpu.VMEM((4, SHARD, LANE), F32),
        pltpu.VMEM((3, SHARD, LANE), F32),
        pltpu.VMEM((SHARD, LANE), BF16),
        pltpu.VMEM((SHARD, LANE), BF16),
        pltpu.VMEM((8, SHARD, LANE), F32),
        pltpu.SemaphoreType.REGULAR,
        pltpu.SemaphoreType.REGULAR,
        pltpu.SemaphoreType.REGULAR,
        pltpu.SemaphoreType.REGULAR,
        pltpu.SemaphoreType.REGULAR,
        dma((8,)),
        dma((NCHUNK,)),
        dma((6,)),
        dma((6,)),
        dma((NCHUNK, 3)),
        dma((NCHUNK, 3)),
        dma((3,)),
        dma((3,)),
        dma((2,)),
        dma((4,)),
        dma((4,)),
        dma((4, 2)),
        dma((4, 2)),
        dma((4, 2)),
        dma((NCHUNK - 1, 3)),
        dma((NCHUNK - 1, 3)),
        dma((PIECES, 3)),
        dma((PIECES, 3)),
        dma((3,)),
        dma((3,)),
        dma((3,)),
        dma((3,)),
        dma((2,)),
        dma((2,)),
        dma((2, 3)),
        dma((2, 3)),
        dma,
        dma,
    ]
    anywhere = pl.BlockSpec(memory_space=pltpu.HBM)
    on_chip = pl.BlockSpec(memory_space=pltpu.VMEM)
    results = pl.pallas_call(
        kernel,
        out_shape=tuple(pltpu.VMEM(shape.shape, shape.dtype) for shape in shapes),
        in_specs=[anywhere] * 7,
        out_specs=[on_chip] * 5,
        scratch_shapes=scratch,
        compiler_params=pltpu.CompilerParams(
            collective_id=0, has_side_effects=True, vmem_limit_bytes=VMEM_LIMIT
        ),
        cost_estimate=pl.CostEstimate(
            flops=4 * ROWS * D * KW, bytes_accessed=16 * 2**20, transcendentals=ROWS
        ),
        name="inner_outer_step",
    )(*args)
    return pl.pallas_call(
        finish,
        out_shape=shapes,
        in_specs=[on_chip] * 5,
        out_specs=[anywhere] * 5,
        scratch_shapes=[pltpu.SemaphoreType.DMA((5,))],
        compiler_params=pltpu.CompilerParams(vmem_limit_bytes=2**20),
        name="write_results",
    )(*(pltpu.with_memory_space_constraint(result, pltpu.VMEM) for result in results))


def solution(mesh):
    return jax.shard_map(
        call,
        mesh=mesh,
        in_specs=(
            P("rep", "fsdp", None),
            P("rep", None),
            P("rep", "fsdp", None),
            P("rep", "fsdp", None),
            P("fsdp", None),
            P("fsdp", None),
            P("rep", "fsdp", None),
        ),
        out_specs=(
            P("rep", "fsdp", None),
            P("rep", None),
            P("rep", "fsdp", None),
            P("fsdp", None),
            P("fsdp", None),
        ),
        check_vma=False,
    )
```

```python
import jax
import jax.numpy as jnp
from jax import lax
from jax.experimental import pallas as pl
from jax.experimental.pallas import tpu as pltpu
from jax.sharding import PartitionSpec as P

EPSILON = 1e-06
OUTER_RATE = 0.7
MOMENTUM = 0.9

MESH = pl.DeviceIdType.MESH
F32 = jnp.float32
BF16 = jnp.bfloat16

D = 4608
KW = 1024
ROWS = 256
SHARD = 288
BLOCK = 1152
CHUNK = 384
NCHUNK = 3
REPS = 16
PIECES = 8
PIECE = ROWS // PIECES
HALF = ROWS // 2
PART = SHARD // 2
LANE = 128
VMEM_LIMIT = 44 * 2**20

WITH_FSDP = True
WITH_REP = True


def input_rows(fin, tok_v, rs_own, gain_v, first, target, to):
    rows = pl.ds(first, 16)
    root = rs_own[rows, :]

    def terms(s, t, q):
        at = s * BLOCK + t * CHUNK + q * LANE
        grad = fin[s, t, rows, q * LANE : (q + 1) * LANE].astype(F32)
        unit = tok_v[rows, at : at + LANE].astype(F32) * root
        return at, grad * (1.0 + gain_v[0:1, at : at + LANE]), unit

    places = [(s, t, q) for s in range(4) for t in range(NCHUNK) for q in range(CHUNK // LANE)]
    total = jnp.zeros((16, LANE), F32)
    for place in places:
        _, scaled, unit = terms(*place)
        total = total + scaled * unit
    projected = jnp.sum(total, axis=1, keepdims=True) / D
    for place in places:
        at, scaled, unit = terms(*place)
        target[pl.ds(to, 16), at : at + LANE] = (root * (scaled - unit * projected)).astype(BF16)


def kernel(
    tokens,
    gain,
    weight,
    cotangent,
    outer,
    momentum,
    inner,
    ig_v,
    wg_v,
    no_v,
    nm_v,
    fin,
    tok_v,
    rs_own,
    gain_v,
    gy,
    cx,
    wx,
    tx,
    rsx,
    rb,
    nt,
    gp,
    sb,
    ru,
    rd,
    fx,
    gz,
    outer_v,
    mom_v,
    inner_v,
    db,
    cr,
    s1,
    xr,
    zs,
    zr,
    xs,
    near_z,
    far_z,
    all_x,
    one_h,
    one_core,
    loc,
    tok_loc,
    c_s,
    c_r,
    t_s,
    t_r,
    r_s,
    r_r,
    w_s,
    w_f,
    w_r,
    g_s,
    u_r,
    d_r,
    f_s,
    f_r,
    p_s,
    p_r,
    gz_s,
    gz_r,
    gy_s,
    gy_r,
    k_s,
    k_r,
    x_s,
    x_r,
    h_s,
    h_r,
):
    fi = lax.axis_index("fsdp")
    ri = lax.axis_index("rep")
    y, z = fi // 4, lax.rem(fi, 4)
    x, zh, core = ri // 4, lax.rem(ri // 2, 2), lax.rem(ri, 2)

    def y_peer(d):
        return (ri, lax.rem(y + d, 4) * 4 + z)

    def z_peer(to):
        return (ri, y * 4 + to)

    def x_peer(d):
        return (lax.rem(x + d, 4) * 4 + zh * 2 + core, fi)

    h_peer = (x * 4 + (1 - zh) * 2 + core, fi)
    core_peer = (x * 4 + zh * 2 + (1 - core), fi)

    def remote(src, dst, send, recv, peer):
        return pltpu.make_async_remote_copy(
            src_ref=src, dst_ref=dst, send_sem=send, recv_sem=recv, device_id=peer, device_id_type=MESH
        )

    def local(src, dst, sem):
        copy = pltpu.make_async_copy(src, dst, sem)
        copy.start()
        return copy

    def chunk_at(step):
        return jnp.where(z < 2, NCHUNK - 1 - step, step)

    def chunk_columns(block, chunk):
        return pl.ds(pl.multiple_of(block * BLOCK + chunk * CHUNK, LANE), CHUNK)

    def shard_rows(j):
        return pl.ds(pl.multiple_of(j * SHARD, 32), SHARD)

    barrier = pltpu.get_barrier_semaphore()
    expected = 0

    def arrive(peer):
        pl.semaphore_signal(barrier, inc=1, device_id=peer, device_id_type=MESH)

    def answer(sem, peer):
        pl.semaphore_signal(sem, inc=1, device_id=peer, device_id_type=MESH)

    if WITH_FSDP:
        for d in (1, 2, 3):
            arrive(y_peer(d))
        for d in (1, 2, 3):

            @pl.when(z + d <= 3)
            def _():
                arrive(z_peer(lax.rem(z + d, 4)))

        expected = expected + 3 + z
    if WITH_REP:
        for d in (1, 2, 3):

            @pl.when(x + d <= 3)
            def _():
                arrive(x_peer(d))

        @pl.when(zh == 0)
        def _():
            arrive(h_peer)

        @pl.when(core == 1)
        def _():
            arrive(core_peer)

        expected = expected + x + zh + (1 - core)
    copies = {}
    if WITH_FSDP:
        copies["tokens"] = local(tokens.at[0], tok_v, loc.at[0])
    if WITH_REP:
        copies["outer"] = local(outer, outer_v, loc.at[4])
        copies["inner"] = local(inner.at[0], inner_v, loc.at[6])

    pl.semaphore_wait(barrier, expected)

    def answers():
        if WITH_FSDP:

            @pl.when(z >= 1)
            def _():
                answer(near_z, z_peer(jnp.maximum(z - 1, 0)))

            for d in (2, 3):

                @pl.when(z >= d)
                def _():
                    answer(far_z, z_peer(jnp.maximum(z - d, 0)))

        if WITH_REP:
            for d in (1, 2, 3):

                @pl.when(x >= d)
                def _():
                    answer(all_x, x_peer(4 - d))

            @pl.when(zh == 1)
            def _():
                answer(one_h, h_peer)

            @pl.when(core == 0)
            def _():
                answer(one_core, core_peer)

    sends = []

    def start(copy):
        copy.start()
        sends.append(copy)
        return copy

    def c_copy(i):
        first, second = pl.ds(0, HALF), pl.ds(HALF, HALF)
        if i < 4:
            rows = first if i in (0, 3) else second
            at = cx.at[y, rows]
            return remote(cotangent.at[0, rows], at, c_s.at[i], c_r.at[i], y_peer(1 if i in (0, 2) else 3))
        if i == 4:
            part = cx.at[lax.rem(y + 3, 4), first]
            return remote(part, part, c_s.at[4], c_r.at[4], y_peer(1))
        part = cx.at[lax.rem(y + 1, 4), second]
        return remote(part, part, c_s.at[5], c_r.at[5], y_peer(3))

    def t_copy(step, d):
        chunk = chunk_at(step)
        return remote(
            tokens.at[0, :, chunk_columns(lax.rem(y + d, 4), chunk)],
            tx.at[chunk, y],
            t_s.at[step, d - 1],
            t_r.at[step, d - 1],
            y_peer(d),
        )

    def r_copy(d):
        return remote(rsx.at[y], rsx.at[y], r_s.at[d - 1], r_r.at[d - 1], y_peer(d))

    up, down = jnp.minimum(z + 1, 3), jnp.maximum(z - 1, 0)

    def w_own(i):
        to = up if i == 0 else down
        return remote(weight.at[0], wx.at[shard_rows(z)], w_s.at[i], w_r.at[z], z_peer(to))

    def w_forward(j, to):
        rows = wx.at[shard_rows(j)]
        return remote(rows, rows, w_f.at[j], w_r.at[j], z_peer(to))

    def weight_step(s):
        @pl.when(z >= s)
        def _():
            w_forward(z - s, up).wait_recv()

            @pl.when(z < 3)
            def _():
                w_forward(z - s, up).start()

        @pl.when(z + s <= 3)
        def _():
            w_forward(z + s, down).wait_recv()

            @pl.when(z > 0)
            def _():
                w_forward(z + s, down).start()

    def g_up(j, part):
        at = (j, pl.ds(part * PART, PART))
        return remote(sb.at[at], ru.at[at], g_s.at[j, part], u_r.at[j, part], z_peer(up))

    def g_down(j, part):
        at = (j, pl.ds(part * PART, PART))
        return remote(sb.at[at], rd.at[at], g_s.at[j, part], d_r.at[j, part], z_peer(down))

    def send_sum(j, part, arrived, copy, first):
        def add(i, _):
            at = part * PART + i * 16
            rows = pl.ds(pl.multiple_of(at, 16), 16)
            total = gp[pl.ds(pl.multiple_of(j * SHARD + at, 16), 16), :]
            if not first:
                total = total + arrived[j, rows, :].astype(F32)
            sb[j, rows, :] = total.astype(BF16)
            return 0

        if not first:
            copy(j, part).wait_recv()
        lax.fori_loop(0, PART // 16, add, 0)
        copy(j, part).start()

    def begin_sums(step):
        @pl.when(z == 0)
        def _():
            for part in range(2):
                send_sum(3 - step, part, ru, g_up, True)

        @pl.when(z == 3)
        def _():
            for part in range(2):
                send_sum(step, part, rd, g_down, True)

    def pass_sums(step, part):
        routes = (((3, ru, g_up), (0, rd, g_down)), ((0, rd, g_down), (3, ru, g_up)), ((2, ru, g_up), (1, rd, g_down)))
        for at, (j, arrived, copy) in zip((1, 2), routes[step]):

            @pl.when(z == at)
            def _():
                send_sum(j, part, arrived, copy, False)

    def end_sums(part):
        @pl.when(z > 0)
        def _():
            g_up(z, part).wait_recv()

        @pl.when(z < 3)
        def _():
            g_down(z, part).wait_recv()

        def add(i, _):
            at = part * PART + i * 16
            rows = pl.ds(pl.multiple_of(at, 16), 16)
            wg_v[0, rows, :] = gp[pl.ds(pl.multiple_of(z * SHARD + at, 16), 16), :]

            @pl.when(z > 0)
            def _():
                wg_v[0, rows, :] += ru[z, rows, :].astype(F32)

            @pl.when(z < 3)
            def _():
                wg_v[0, rows, :] += rd[z, rows, :].astype(F32)

            return 0

        lax.fori_loop(0, PART // 16, add, 0)

    def feature_chunk(step):
        return jnp.where(z < 2, step, NCHUNK - 1 - step)

    def f_copy(step, d):
        chunk = feature_chunk(step)
        to = lax.rem(y + d, 4)
        return remote(fx.at[chunk, to], fin.at[y, chunk], f_s.at[step, d - 1], f_r.at[step, d - 1], y_peer(d))

    def p_copy(piece, d):
        chunk = feature_chunk(NCHUNK - 1)
        to = lax.rem(y + d, 4)
        rows = pl.ds(pl.multiple_of(piece * PIECE, 16), PIECE)
        return remote(
            fx.at[chunk, to, rows], fin.at[y, chunk, rows], p_s.at[piece, d - 1], p_r.at[piece, d - 1], y_peer(d)
        )

    def gz_copy(d):
        return remote(gz.at[z], gz.at[z], gz_s.at[d - 1], gz_r.at[d - 1], z_peer(lax.rem(z + d, 4)))

    def gy_copy(d):
        return remote(gy.at[y], gy.at[y], gy_s.at[d - 1], gy_r.at[d - 1], y_peer(d))

    def k_copy(i):
        if i == 0:
            return remote(db.at[pl.ds((1 - core) * 4, 4)], cr, k_s.at[0], k_r.at[0], core_peer)
        part = xs.at[pl.ds(core * 4, 4)]
        return remote(part, part, k_s.at[1], k_r.at[1], core_peer)

    def x_copy(i, d):
        if i == 0:
            return remote(
                s1.at[lax.rem(x + d, 4)], xr.at[d - 1], x_s.at[0, d - 1], x_r.at[0, d - 1], x_peer(d)
            )
        part = xs.at[core * 4 + x]
        return remote(part, part, x_s.at[1, d - 1], x_r.at[1, d - 1], x_peer(d))

    def h_copy():
        return remote(zs, zr, h_s, h_r, h_peer)

    def inverse_root():
        def body(i, _):
            rows = pl.ds(pl.multiple_of(i * 16, 16), 16)
            total = jnp.zeros((16, LANE), F32)
            for j in range(D // LANE):
                v = tok_v[rows, j * LANE : (j + 1) * LANE].astype(F32)
                total = total + v * v
            mean = jnp.sum(total, axis=1, keepdims=True) / D
            rs_own[rows, :] = jnp.broadcast_to(lax.rsqrt(mean + EPSILON), (16, LANE))
            return 0

        lax.fori_loop(0, ROWS // 16, body, 0)
        rsx[y] = jnp.transpose(rs_own[...])[0:8, :]

    def spread_roots():
        def body(s, _):
            rb[s] = jnp.transpose(jnp.broadcast_to(rsx[s][0:1, :], (LANE, ROWS)))
            return 0

        lax.fori_loop(0, 4, body, 0)

    def weight_chunk(chunk):
        def norm(s, _):
            for q in range(CHUNK // LANE):
                unit = tx[chunk, s, :, q * LANE : (q + 1) * LANE].astype(F32) * rb[s]
                at = pl.multiple_of(y * BLOCK + chunk * CHUNK + q * LANE, LANE)
                normed = (unit * (1.0 + gain_v[0:1, pl.ds(at, LANE)])).astype(BF16)
                nt[s, q * LANE : (q + 1) * LANE, :] = jnp.transpose(normed)
            return 0

        lax.fori_loop(0, 4, norm, 0)

        def multiply(j, _):
            columns = pl.ds(pl.multiple_of(j * 256, 256), 256)
            total = jnp.zeros((CHUNK, 256), F32)
            for s in range(4):
                total = total + jnp.dot(nt[s], cx[s, :, columns], preferred_element_type=F32)
            gp[pl.ds(pl.multiple_of(chunk * CHUNK, CHUNK), CHUNK), columns] = total
            return 0

        lax.fori_loop(0, KW // 256, multiply, 0)

    def features(step):
        chunk = feature_chunk(step)
        rows = pl.ds(pl.multiple_of(chunk * CHUNK, CHUNK), CHUNK)

        def body(s, _):
            product = lax.dot_general(cx[s], wx[rows, :], (((1,), (1,)), ((), ())), preferred_element_type=F32)
            fx[chunk, s] = product.astype(BF16)
            return 0

        lax.fori_loop(0, 4, body, 0)

    def gain_part():
        gz[z] = jnp.zeros((16, LANE), F32)

        def body(t, _):
            for q in range(CHUNK // LANE):
                lanes = slice(q * LANE, (q + 1) * LANE)

                def add(s, total):
                    unit = tx[t, s, :, lanes].astype(F32) * rb[s]
                    term = fx[t, s, :, lanes].astype(F32) * unit
                    return total + jnp.sum(term.reshape(ROWS // 8, 8, LANE), axis=0)

                total = lax.fori_loop(0, 4, add, jnp.zeros((8, LANE), F32))
                gz[z, pl.ds(t * (CHUNK // LANE) + q, 1), :] = jnp.sum(total, axis=0, keepdims=True)
            return 0

        lax.fori_loop(0, NCHUNK, body, 0)

    def input_piece(piece):
        def body(i, _):
            at = pl.multiple_of(piece * PIECE + i * 16, 16)
            input_rows(fin, tok_v, rs_own, gain_v, at, ig_v.at[0], at)
            return 0

        lax.fori_loop(0, PIECE // 16, body, 0)

    if WITH_FSDP:
        for i in range(4):
            start(c_copy(i))

        @pl.when(z > 0)
        def _():
            w_own(1).start()

        for d in (1, 3, 2):
            start(t_copy(0, d))

        answers()

        copies["gain"] = local(gain, gain_v, loc.at[1])
        copies["c"] = local(cotangent.at[0], cx.at[y], loc.at[2])
        copies["w"] = local(weight.at[0], wx.at[shard_rows(z)], loc.at[3])
        for step in range(NCHUNK):
            chunk = chunk_at(step)
            copies["t", step] = local(
                tokens.at[0, :, chunk_columns(y, chunk)], tx.at[chunk, y], tok_loc.at[step]
            )
    if WITH_REP:
        copies["momentum"] = local(momentum, mom_v, loc.at[5])
    if not WITH_FSDP:
        answers()
    if WITH_FSDP:

        @pl.when(z < 3)
        def _():
            pl.semaphore_wait(near_z, 1)
            w_own(0).start()

    if WITH_REP:
        copies["outer"].wait()
        copies["inner"].wait()

        def differ(b, _):
            lanes = pl.ds(pl.multiple_of(b * LANE, LANE), LANE)
            db[b] = outer_v[:, lanes] - inner_v[:, lanes].astype(F32)
            return 0

        lax.fori_loop(0, 8, differ, 0)

        @pl.when(core == 1)
        def _():
            pl.semaphore_wait(one_core, 1)

        start(k_copy(0))

    if WITH_FSDP:
        copies["tokens"].wait()
        inverse_root()
        for d in (1, 3, 2):
            start(r_copy(d))
        c_copy(0).wait_recv()
        start(c_copy(4))
        c_copy(1).wait_recv()
        start(c_copy(5))
        for step in range(1, NCHUNK):
            for d in (1, 3, 2):
                start(t_copy(step, d))

    if WITH_REP:
        k_copy(0).wait_recv()
        for q in range(4):
            s1[q] = db[core * 4 + q] + cr[q]

        @pl.when(x < 3)
        def _():
            pl.semaphore_wait(all_x, 3 - x)

        for d in (1, 2, 3):
            start(x_copy(0, d))

    if WITH_FSDP:
        weight_step(1)

    if WITH_REP:
        for d in (1, 2, 3):
            x_copy(0, d).wait_recv()
        zs[...] = (s1[x] + xr[0] + xr[1] + xr[2]).astype(BF16)

        @pl.when(zh == 0)
        def _():
            pl.semaphore_wait(one_h, 1)

        start(h_copy())

    if WITH_FSDP:
        copies["gain"].wait()
        for d in (1, 2, 3):
            r_copy(d).wait_recv()
        spread_roots()
        copies["c"].wait()
        for i in range(2, 6):
            c_copy(i).wait_recv()
        copies["t", 0].wait()
        for d in (1, 2, 3):
            t_copy(0, d).wait_recv()
        weight_chunk(chunk_at(0))
        begin_sums(0)
        copies["w"].wait()
        weight_step(2)

        def early_features(step, _):
            features(step)
            for d in (1, 3, 2):
                f_copy(step, d).start()
            return 0

        lax.fori_loop(0, NCHUNK - 1, early_features, 0)

    if WITH_REP:
        h_copy().wait_recv()
        xs[core * 4 + x] = zs[...].astype(F32) + zr[...].astype(F32)
        for d in (1, 2, 3):
            start(x_copy(1, d))

    if WITH_FSDP:
        copies["t", 1].wait()
        for d in (1, 2, 3):
            t_copy(1, d).wait_recv()
        weight_chunk(chunk_at(1))
        begin_sums(1)
        pass_sums(0, 0)

    if WITH_REP:
        for d in (1, 2, 3):
            x_copy(1, d).wait_recv()
        start(k_copy(1))

    if WITH_FSDP:
        weight_step(3)
        features(NCHUNK - 1)
        for piece in range(PIECES - 2):
            for d in (1, 3, 2):
                start(p_copy(piece, d))

    if WITH_REP:
        copies["momentum"].wait()
        k_copy(1).wait_recv()

        def nesterov(b, _):
            lanes = pl.ds(pl.multiple_of(b * LANE, LANE), LANE)
            pseudo = xs[b] / REPS
            momentum_next = MOMENTUM * mom_v[:, lanes] + pseudo
            nm_v[:, lanes] = momentum_next
            no_v[:, lanes] = outer_v[:, lanes] - OUTER_RATE * (pseudo + MOMENTUM * momentum_next)
            return 0

        lax.fori_loop(0, 8, nesterov, 0)

    if WITH_FSDP:
        own = local(fx.at[:, y], fin.at[y], loc.at[7])
        pass_sums(0, 1)
        copies["t", 2].wait()
        for d in (1, 2, 3):
            t_copy(2, d).wait_recv()
        gain_part()

        @pl.when(z < 2)
        def _():
            pl.semaphore_wait(far_z, 2 - z)

        for d in (1, 2, 3):
            start(gz_copy(d))
        weight_chunk(chunk_at(2))
        begin_sums(2)
        pass_sums(1, 0)
        pass_sums(2, 0)
        pass_sums(1, 1)
        for d in (1, 2, 3):
            gz_copy(d).wait_recv()
        gy[y] = gz[0] + gz[1] + gz[2] + gz[3]
        for d in (1, 3, 2):
            start(gy_copy(d))
        for piece in range(PIECES - 2, PIECES):
            for d in (1, 3, 2):
                start(p_copy(piece, d))
        pass_sums(2, 1)
        own.wait()
        for step in range(NCHUNK - 1):
            for d in (1, 2, 3):
                f_copy(step, d).wait_recv()

        def last_rows(piece, _):
            for d in (1, 2, 3):
                p_copy(piece, d).wait_recv()
            input_piece(piece)
            return 0

        end_sums(0)
        lax.fori_loop(0, PIECES - 1, last_rows, 0)
        for d in (1, 2, 3):
            p_copy(PIECES - 1, d).wait_recv()
        end_sums(1)
        for d in (1, 2, 3):
            gy_copy(d).wait_recv()

    for copy in sends:
        copy.wait_send()
    if WITH_FSDP:
        for step in range(NCHUNK - 1):
            for d in (1, 2, 3):
                f_copy(step, d).wait_send()

        @pl.when(z < 3)
        def _():
            w_own(0).wait_send()

        @pl.when(z > 0)
        def _():
            w_own(1).wait_send()

        for s in (1, 2):

            @pl.when((z >= s) & (z < 3))
            def _():
                w_forward(z - s, up).wait_send()

            @pl.when((z + s <= 3) & (z > 0))
            def _():
                w_forward(z + s, down).wait_send()

        for d in (1, 2, 3):
            for part in range(2):
                g_up(lax.rem(z + d, 4), part).wait_send()


def finish(
    ig_v, wg_v, no_v, nm_v, fin, tok_v, rs_own, gain_v, gy,
    input_grad, gain_grad, weight_grad, new_outer, new_momentum,
    last_v, gg_v, sems,
):
    done = ROWS - PIECE
    pairs = [
        (ig_v.at[0, pl.ds(0, done)], input_grad.at[0, pl.ds(0, done)]),
        (wg_v, weight_grad),
        (no_v, new_outer),
        (nm_v, new_momentum),
        (last_v, input_grad.at[0, pl.ds(done, PIECE)]),
        (gg_v, gain_grad),
    ]
    copies = [pltpu.make_async_copy(source, target, sems.at[i]) for i, (source, target) in enumerate(pairs)]
    for copy in copies[:4]:
        copy.start()

    def body(i, _):
        at = pl.multiple_of(i * 16, 16)
        input_rows(fin, tok_v, rs_own, gain_v, done + at, last_v, at)
        return 0

    lax.fori_loop(0, PIECE // 16, body, 0)
    copies[4].start()
    for b in range(4):
        for i in range(BLOCK // LANE):
            at = b * BLOCK + i * LANE
            gg_v[0:1, at : at + LANE] = gy[b, i : i + 1, :]
    copies[5].start()
    for copy in copies:
        copy.wait()


def call(tokens, gain, *rest):
    args = (tokens, pltpu.with_memory_space_constraint(gain, pltpu.HBM), *rest)
    shapes = (
        jax.ShapeDtypeStruct((1, ROWS, D), BF16),
        jax.ShapeDtypeStruct((1, D), F32),
        jax.ShapeDtypeStruct((1, SHARD, KW), F32),
        jax.ShapeDtypeStruct((SHARD, KW), F32),
        jax.ShapeDtypeStruct((SHARD, KW), F32),
    )
    held = (
        pltpu.VMEM((1, ROWS, D), BF16),
        pltpu.VMEM((1, SHARD, KW), F32),
        pltpu.VMEM((SHARD, KW), F32),
        pltpu.VMEM((SHARD, KW), F32),
        pltpu.VMEM((4, NCHUNK, ROWS, CHUNK), BF16),
        pltpu.VMEM((ROWS, D), BF16),
        pltpu.VMEM((ROWS, LANE), F32),
        pltpu.VMEM((1, D), F32),
        pltpu.VMEM((4, 16, LANE), F32),
    )
    dma = pltpu.SemaphoreType.DMA
    scratch = [
        pltpu.VMEM((4, ROWS, KW), BF16),
        pltpu.VMEM((BLOCK, KW), BF16),
        pltpu.VMEM((NCHUNK, 4, ROWS, CHUNK), BF16),
        pltpu.VMEM((4, 8, ROWS), F32),
        pltpu.VMEM((4, ROWS, LANE), F32),
        pltpu.VMEM((4, CHUNK, ROWS), BF16),
        pltpu.VMEM((BLOCK, KW), F32),
        pltpu.VMEM((4, SHARD, KW), BF16),
        pltpu.VMEM((4, SHARD, KW), BF16),
        pltpu.VMEM((4, SHARD, KW), BF16),
        pltpu.VMEM((NCHUNK, 4, ROWS, CHUNK), BF16),
        pltpu.VMEM((4, 16, LANE), F32),
        pltpu.VMEM((SHARD, KW), F32),
        pltpu.VMEM((SHARD, KW), F32),
        pltpu.VMEM((SHARD, KW), BF16),
        pltpu.VMEM((8, SHARD, LANE), F32),
        pltpu.VMEM((4, SHARD, LANE), F32),
        pltpu.VMEM((4, SHARD, LANE), F32),
        pltpu.VMEM((3, SHARD, LANE), F32),
        pltpu.VMEM((SHARD, LANE), BF16),
        pltpu.VMEM((SHARD, LANE), BF16),
        pltpu.VMEM((8, SHARD, LANE), F32),
        pltpu.SemaphoreType.REGULAR,
        pltpu.SemaphoreType.REGULAR,
        pltpu.SemaphoreType.REGULAR,
        pltpu.SemaphoreType.REGULAR,
        pltpu.SemaphoreType.REGULAR,
        dma((8,)),
        dma((NCHUNK,)),
        dma((6,)),
        dma((6,)),
        dma((NCHUNK, 3)),
        dma((NCHUNK, 3)),
        dma((3,)),
        dma((3,)),
        dma((2,)),
        dma((4,)),
        dma((4,)),
        dma((4, 2)),
        dma((4, 2)),
        dma((4, 2)),
        dma((NCHUNK - 1, 3)),
        dma((NCHUNK - 1, 3)),
        dma((PIECES, 3)),
        dma((PIECES, 3)),
        dma((3,)),
        dma((3,)),
        dma((3,)),
        dma((3,)),
        dma((2,)),
        dma((2,)),
        dma((2, 3)),
        dma((2, 3)),
        dma,
        dma,
    ]
    anywhere = pl.BlockSpec(memory_space=pltpu.HBM)
    on_chip = pl.BlockSpec(memory_space=pltpu.VMEM)
    results = pl.pallas_call(
        kernel,
        out_shape=held,
        in_specs=[anywhere] * 7,
        out_specs=[on_chip] * len(held),
        scratch_shapes=scratch,
        compiler_params=pltpu.CompilerParams(
            collective_id=0, has_side_effects=True, vmem_limit_bytes=VMEM_LIMIT
        ),
        cost_estimate=pl.CostEstimate(
            flops=4 * ROWS * D * KW, bytes_accessed=16 * 2**20, transcendentals=ROWS
        ),
        name="inner_outer_step",
    )(*args)
    return pl.pallas_call(
        finish,
        out_shape=shapes,
        in_specs=[on_chip] * len(held),
        out_specs=[anywhere] * 5,
        scratch_shapes=[pltpu.VMEM((PIECE, D), BF16), pltpu.VMEM((1, D), F32), pltpu.SemaphoreType.DMA((6,))],
        compiler_params=pltpu.CompilerParams(vmem_limit_bytes=2**22),
        name="write_results",
    )(*(pltpu.with_memory_space_constraint(result, pltpu.VMEM) for result in results))


def solution(mesh):
    return jax.shard_map(
        call,
        mesh=mesh,
        in_specs=(
            P("rep", "fsdp", None),
            P("rep", None),
            P("rep", "fsdp", None),
            P("rep", "fsdp", None),
            P("fsdp", None),
            P("fsdp", None),
            P("rep", "fsdp", None),
        ),
        out_specs=(
            P("rep", "fsdp", None),
            P("rep", None),
            P("rep", "fsdp", None),
            P("fsdp", None),
            P("fsdp", None),
        ),
        check_vma=False,
    )
```
